128 devices in a mesh: ctx: 32 (over z, y, core), ch: 4 (over x).
Axes of the slice: x: 4, y: 4, z: 4, core: 2. Of those that a mesh axis runs over, the one named last changes fastest.
Arguments:
- q_in: bfloat16 [16384, 4096], P('ctx', 'ch'), may hold values from -6 to 6
- k_in: bfloat16 [16384, 4096], P('ctx', 'ch'), may hold values from -6 to 6
- v_in: bfloat16 [16384, 4096], P('ctx', 'ch'), may hold values from -6 to 6
- out_grad: bfloat16 [16384, 4096], P('ctx', 'ch'), may hold values from -6 to 6
- filters: float32 [16384, 1024], P('ctx'), may hold values from -1.5 to 1.5
- skip: float32 [4096], P('ch'), may hold values from 0.5 to 2
Outputs:
- q_grad: bfloat16 [16384, 4096], P('ctx', 'ch')
- k_grad: bfloat16 [16384, 4096], P('ctx', 'ch')
- v_grad: bfloat16 [16384, 4096], P('ctx', 'ch')
- filter_grad: float32 [16384, 1024], P('ctx', 'ch')
The draws below stay inside these ranges and needn't reach their ends.
All inputs are finite; a program needn't handle non-finite values.
Results may differ from the reference program's by a relative error of at most 0.007.
Values may be sent and summed in bfloat16 or wider, within the bound.
No kernel may reach another device: no remote copies, remote signals or barrier semaphores. Data moves between devices by JAX's collectives and lax.ppermute only.
A program may use at most 192 MiB of HBM per device.

```python
import math
import jax
import jax.numpy as jnp
from jax import lax

L_DEV = 512
CH = 4096
TOKENS = 16384
FILTERS = 1024
N_CTX = 32


def draw_filters(key, part):
    key = jax.random.fold_in(key, 7)
    key_pick = jax.random.fold_in(key, 1)
    key_fast = jax.random.fold_in(key, 2)
    key_slow = jax.random.fold_in(key, 3)
    key_value = jax.random.fold_in(key, 4)
    slow_share = 0.5
    picked = jax.random.uniform(key_pick, (FILTERS,), jnp.float32) < slow_share
    fast_tau = jnp.exp(jax.random.uniform(key_fast, (FILTERS,), jnp.float32, math.log(16.0), math.log(48.0)))
    slow_tau = jnp.exp(jax.random.uniform(key_slow, (FILTERS,), jnp.float32, math.log(0.5 * TOKENS), math.log(4.0 * TOKENS)))
    decay_tau = jnp.where(picked, slow_tau, fast_tau)
    position = jnp.arange(TOKENS, dtype=jnp.float32)
    envelope = jnp.exp(-position[:, None] / decay_tau[None, :]) / jnp.sqrt(decay_tau)[None, :]
    noise = jax.random.truncated_normal(key_value, -4.0, 4.0, (TOKENS, FILTERS), jnp.float32)
    return (1.4 * noise * envelope).astype(jnp.float32)


def level_of(stream_key, shape, cuts, least, high):
    level, own = 1.0, jax.random.fold_in(stream_key, 6)
    for dim, shards_of in cuts:
        heights = jnp.exp(jax.random.uniform(jax.random.fold_in(own, dim), (shards_of,), jnp.float32, least / len(cuts), high / len(cuts)))
        level = level * jnp.repeat(heights, shape[dim] // shards_of).reshape([-1 if axis == dim else 1 for axis in range(len(shape))])
    return level


def centred(key, extent, spread, bound, pieces=(), kind=jnp.bfloat16):
    entries = jax.random.normal(key, extent, jnp.float32) * spread
    if len(pieces) > 0:
        entries = level_of(key, extent, pieces, -0.22, 0.18) * entries
    return jnp.clip(entries, min=-bound, max=bound).astype(kind)


def setup_inputs(seed: int = 0) -> dict:
    key_of = jax.random.split(jax.random.key(seed), 7)
    q_in = centred(key_of[0], (TOKENS, CH), 1.0, 6.0, ((0, 32), (1, 4)))
    k_in = centred(key_of[1], (TOKENS, CH), 1.0, 6.0, ((0, 32), (1, 4)))
    v_in = centred(key_of[2], (TOKENS, CH), 1.0, 6.0, ((0, 32), (1, 4)))
    out_grad = centred(key_of[3], (TOKENS, CH), 1.0, 6.0, ((0, 32), (1, 4)))
    filters = draw_filters(jax.random.fold_in(key_of[6], 71), 0)
    skip = jnp.clip(jnp.exp(math.log(2.0) - 1.3862944 * jax.random.uniform(key_of[5], (CH,), jnp.float32) ** level_of(key_of[5], (CH,), ((0, 4),), -0.2, 0.2)), 0.5, 2.0)
    return {"q_in": q_in, "k_in": k_in, "v_in": v_in, "out_grad": out_grad, "filters": filters, "skip": skip}


def phase_table(left_index, right_index, period):
    product = left_index[:, None] * right_index[None, :] % period
    angle = product.astype(jnp.float32) * (2.0 * math.pi / period)
    return (jnp.cos(angle), jnp.sin(angle))

def multiply(form, table, data):
    return jnp.einsum(form, table.astype(jnp.float32), data.astype(jnp.float32), precision=lax.Precision.HIGHEST)

def forward_spec(field_low):
    width = field_low.shape[1]
    period = 2 * TOKENS
    blocks = field_low.reshape(N_CTX, L_DEV, width)
    frequency = jnp.arange(2 * N_CTX, dtype=jnp.int32)
    cos_block, sin_block = phase_table(frequency, jnp.arange(N_CTX, dtype=jnp.int32), 2 * N_CTX)
    cos_block = cos_block.astype(jnp.bfloat16)
    sin_block = sin_block.astype(jnp.bfloat16)
    real_part = multiply('ka,ajc->kjc', cos_block, blocks)
    imag_part = -multiply('ka,ajc->kjc', sin_block, blocks)
    cos_twist, sin_twist = phase_table(frequency, jnp.arange(L_DEV, dtype=jnp.int32), period)
    twist_re = (real_part * cos_twist[:, :, None] + imag_part * sin_twist[:, :, None]).astype(jnp.bfloat16)
    twist_im = (imag_part * cos_twist[:, :, None] - real_part * sin_twist[:, :, None]).astype(jnp.bfloat16)
    index_row = jnp.arange(L_DEV, dtype=jnp.int32)
    cos_row, sin_row = phase_table(index_row, index_row, L_DEV)
    cos_row = cos_row.astype(jnp.bfloat16)
    sin_row = sin_row.astype(jnp.bfloat16)
    cos_real = multiply('qj,kjc->kqc', cos_row, twist_re)
    cos_imag = multiply('qj,kjc->kqc', cos_row, twist_im)
    sin_real = multiply('qj,kjc->kqc', sin_row, twist_re)
    sin_imag = multiply('qj,kjc->kqc', sin_row, twist_im)
    return (cos_real + sin_imag, cos_imag - sin_real)

def inverse_spec(spec_re, spec_im, low):
    width = spec_re.shape[2]
    period = 2 * TOKENS
    index_row = jnp.arange(L_DEV, dtype=jnp.int32)
    cos_row, sin_row = phase_table(index_row, index_row, L_DEV)
    frequency = jnp.arange(2 * N_CTX, dtype=jnp.int32)
    cos_block, sin_block = phase_table(jnp.arange(N_CTX, dtype=jnp.int32), frequency, 2 * N_CTX)
    if low:
        spec_re = spec_re.astype(jnp.bfloat16)
        spec_im = spec_im.astype(jnp.bfloat16)
        cos_row = cos_row.astype(jnp.bfloat16)
        sin_row = sin_row.astype(jnp.bfloat16)
        cos_block = cos_block.astype(jnp.bfloat16)
        sin_block = sin_block.astype(jnp.bfloat16)
    row_re = multiply('qj,kjc->kqc', cos_row, spec_re) - multiply('qj,kjc->kqc', sin_row, spec_im)
    row_im = multiply('qj,kjc->kqc', cos_row, spec_im) + multiply('qj,kjc->kqc', sin_row, spec_re)
    cos_twist, sin_twist = phase_table(frequency, jnp.arange(L_DEV, dtype=jnp.int32), period)
    real_part = row_re * cos_twist[:, :, None] - row_im * sin_twist[:, :, None]
    imag_part = row_im * cos_twist[:, :, None] + row_re * sin_twist[:, :, None]
    if low:
        real_part = real_part.astype(jnp.bfloat16)
        imag_part = imag_part.astype(jnp.bfloat16)
    summed = multiply('ak,kjc->ajc', cos_block, real_part) - multiply('ak,kjc->ajc', sin_block, imag_part)
    return (summed * (1.0 / period)).reshape(TOKENS, width)

def reference(q_in, k_in, v_in, out_grad, filters, skip):
    gated_low = (k_in.astype(jnp.float32) * v_in.astype(jnp.float32)).astype(jnp.bfloat16)
    grad_low = (q_in.astype(jnp.float32) * out_grad.astype(jnp.float32)).astype(jnp.bfloat16)
    filters_low = filters.astype(jnp.bfloat16)
    gated = lax.optimization_barrier(gated_low).astype(jnp.float32)
    grad_gated = lax.optimization_barrier(grad_low).astype(jnp.float32)
    filt_re, filt_im = forward_spec(filters_low)
    q_parts = []
    k_parts = []
    v_parts = []
    taps_re = jnp.zeros(filt_re.shape, jnp.float32)
    taps_im = jnp.zeros(filt_re.shape, jnp.float32)
    for group_index in range(CH // FILTERS):
        lower = group_index * FILTERS
        upper = lower + FILTERS
        gated_re, gated_im = forward_spec(gated_low[:, lower:upper])
        grad_re, grad_im = forward_spec(grad_low[:, lower:upper])
        state_re = gated_re * filt_re - gated_im * filt_im
        state_im = gated_re * filt_im + gated_im * filt_re
        back_re = grad_re * filt_re + grad_im * filt_im
        back_im = grad_im * filt_re - grad_re * filt_im
        taps_re = taps_re + (grad_re * gated_re + grad_im * gated_im)
        taps_im = taps_im + (grad_im * gated_re - grad_re * gated_im)
        skip_part = skip[lower:upper]
        mixed_state = inverse_spec(state_re, state_im, True) + skip_part[None, :] * gated[:, lower:upper]
        gated_back = inverse_spec(back_re, back_im, True) + skip_part[None, :] * grad_gated[:, lower:upper]
        q_parts.append((out_grad[:, lower:upper].astype(jnp.float32) * mixed_state).astype(jnp.bfloat16))
        k_parts.append((gated_back * v_in[:, lower:upper].astype(jnp.float32)).astype(jnp.bfloat16))
        v_parts.append((gated_back * k_in[:, lower:upper].astype(jnp.float32)).astype(jnp.bfloat16))
    filter_total = inverse_spec(taps_re, taps_im, False)
    scale_factor = 1.0 / math.sqrt(TOKENS * (CH // FILTERS))
    filter_grad = (filter_total * scale_factor).astype(jnp.float32)
    return (jnp.concatenate(q_parts, axis=1), jnp.concatenate(k_parts, axis=1), jnp.concatenate(v_parts, axis=1), filter_grad)
```

```python
import functools
import math

import jax
import jax.numpy as jnp
import ml_dtypes
import numpy as np
from jax import lax
from jax.experimental import pallas as pl
from jax.experimental.pallas import tpu as pltpu
from jax.sharding import PartitionSpec as P

BF = jnp.bfloat16
F32 = jnp.float32

A = 32
X = 4
DEV = A * X
L = 128
SEG = 4 * L
KH = A + 1
PERIOD = 2 * A * SEG
ROWS = 72
MIB = 1024 * 1024


def low(table):
    return np.asarray(table, np.float32).astype(ml_dtypes.bfloat16)


def spread(table, count):
    return np.kron(table, np.eye(count))


@functools.cache
def constants():
    k = np.arange(KH)[:, None]
    a = np.arange(A)[None, :]
    angle = 2 * np.pi * (k * a % (2 * A)) / (2 * A)
    cos_block = low(np.cos(angle)).astype(np.float64)
    sin_block = low(np.sin(angle)).astype(np.float64)
    cos_block[np.abs(cos_block) < 1e-6] = 0.0
    sin_block[np.abs(sin_block) < 1e-6] = 0.0
    forward = np.concatenate([cos_block, -sin_block], 0)
    weight = np.where((k == 0) | (k == A), 1.0, 2.0) / PERIOD
    backward = np.concatenate([weight * cos_block, -(weight * sin_block)[1:A]], 0).T
    l = np.arange(L)[:, None]
    fwd_rows, inv_rows = [], []
    for r in range(4):
        q = r + 4 * np.arange(L)[None, :]
        angle = 2 * np.pi * (l * q % SEG) / SEG
        c, s = np.cos(angle), np.sin(angle)
        fwd_rows.append(np.block([[c, -s], [s, c]]))
        inv_rows.append(np.block([[c.T, s.T], [-s.T, c.T]]))
    j = np.arange(SEG)[None, :]
    twist = 2 * np.pi * (k * j % PERIOD) / PERIOD
    row = np.arange(512)
    column = (row // 2) % 4 * 128 + row // 8 * 2 + row % 2
    order = np.zeros((512, 512))
    order[row, column] = 1.0
    return {
        "fwd_pair": low(spread(forward, 16)),
        "fwd_one": low(spread(forward, 8)),
        "inv_pair": low(spread(backward, 16)),
        "inv_one": low(spread(backward / 256.0, 8)),
        "fwd_rows": low(np.stack(fwd_rows)),
        "inv_rows": low(np.stack(inv_rows)),
        "cos_twist": np.cos(twist).astype(np.float32),
        "sin_twist": np.sin(twist).astype(np.float32),
        "order": low(order),
    }


def mm(left, right):
    return jnp.dot(left, right, preferred_element_type=F32)


def up(value):
    return value.astype(F32)


def whole():
    return pl.BlockSpec(memory_space=pltpu.VMEM)


def pack_kernel(index_ref, q_ref, k_ref, v_ref, o_ref, f_ref, order_ref, out_ref):
    step = pl.program_id(0)
    gated = (up(k_ref[...]) * up(v_ref[...])).astype(BF)
    grad = (up(q_ref[...]) * up(o_ref[...])).astype(BF)
    both = jnp.concatenate([gated, grad], axis=0)

    def by_owner(field, half):
        columns = jnp.concatenate(
            [field[:, g * 256 + half * 128 : g * 256 + half * 128 + 128] for g in range(4)], axis=1
        )
        return lax.dot_general(
            order_ref[...], columns, (((1,), (1,)), ((), ())), preferred_element_type=F32
        )

    for half in range(2):
        rows = by_owner(both, half)
        pair = jnp.concatenate(
            [rows[:, :L].reshape(64, 8, L), rows[:, L:].reshape(64, 8, L)], axis=1
        )
        out_ref[half * 64 : half * 64 + 64, pl.ds(pl.multiple_of(step * 16, 16), 16), :] = (
            pair.astype(BF)
        )

    @pl.when(step == 0)
    def _():
        taps = f_ref[...].astype(BF)
        for half in range(2):
            rows = by_owner(taps, half).reshape(64, 8, L)
            out_ref[half * 64 : half * 64 + 64, 64:72, :] = rows.astype(BF)


def pack(index, q_in, k_in, v_in, out_grad, filters, order):
    field = pl.BlockSpec((L, 1024), lambda i, s: (i, 0))
    return pl.pallas_call(
        pack_kernel,
        out_shape=jax.ShapeDtypeStruct((DEV, ROWS, L), BF),
        grid_spec=pltpu.PrefetchScalarGridSpec(
            num_scalar_prefetch=1,
            grid=(4,),
            in_specs=[field] * 4
            + [
                pl.BlockSpec((L, 1024), lambda i, s: (s[0], 0)),
                pl.BlockSpec((512, 512), lambda i, s: (0, 0)),
            ],
            out_specs=pl.BlockSpec((DEV, ROWS, L), lambda i, s: (0, 0, 0)),
        ),
        compiler_params=pltpu.CompilerParams(vmem_limit_bytes=40 * MIB),
        name="pack",
    )(index, q_in, k_in, v_in, out_grad, filters, order)


def quarters(value):
    return [value[:, i * L : (i + 1) * L] for i in range(4)]


def butterfly(re, im, sign):
    ar, br, cr, dr = re[0] + re[2], re[0] - re[2], re[1] + re[3], re[1] - re[3]
    ai, bi, ci, di = im[0] + im[2], im[0] - im[2], im[1] + im[3], im[1] - im[3]
    plus = (br - di, bi + dr)
    minus = (br + di, bi - dr)
    first, third = (plus, minus) if sign > 0 else (minus, plus)
    return [(ar + cr, ai + ci), first, (ar - cr, ai - ci), third]


def twist_forward(sums_ref, cos_ref, sin_ref, out_ref, height):
    for k in range(KH):
        re = sums_ref[k * height : (k + 1) * height, :]
        im = sums_ref[(KH + k) * height : (KH + k + 1) * height, :]
        c = cos_ref[k : k + 1, :]
        s = sin_ref[k : k + 1, :]
        parts = butterfly(quarters(re * c + im * s), quarters(im * c - re * s), -1)
        for n, (zr, zi) in enumerate(parts):
            rows = slice(k * height, (k + 1) * height)
            out_ref[rows, n * 256 : n * 256 + L] = zr.astype(BF)
            out_ref[rows, n * 256 + L : n * 256 + 256] = zi.astype(BF)


def rows_of(data_ref, table_ref, out_ref, height):
    for n in range(4):
        cols = slice(n * 256, (n + 1) * 256)
        out_ref[: KH * height, cols] = mm(data_ref[: KH * height, cols], table_ref[n])


def twist_back(rows_ref, cos_ref, sin_ref, out_ref, height):
    for k in range(KH):
        rows = slice(k * height, (k + 1) * height)
        re = [rows_ref[rows, n * 256 : n * 256 + L] for n in range(4)]
        im = [rows_ref[rows, n * 256 + L : n * 256 + 256] for n in range(4)]
        for n, (ur, ui) in enumerate(butterfly(re, im, 1)):
            cols = slice(n * L, (n + 1) * L)
            c = cos_ref[k : k + 1, cols]
            s = sin_ref[k : k + 1, cols]
            out_ref[rows, cols] = (ur * c - ui * s).astype(BF)
            if 0 < k < A:
                lower = (KH + k - 1) * height
                out_ref[lower : lower + height, cols] = (ui * c + ur * s).astype(BF)


def transform_kernel(
    in_ref, fp_ref, fo_ref, ip_ref, io_ref, fr_ref, ir_ref, cos_ref, sin_ref, out_ref,
    sums_ref, z_ref, spec_ref, y_ref, u_ref, filt_ref, taps_ref,
):
    taps_in = jnp.concatenate(
        [up(in_ref[:, g, 64:72, :]).reshape(A * 8, L) for g in range(4)], axis=1
    ).astype(BF)
    sums_ref[: 2 * KH * 8, :] = mm(fo_ref[...], taps_in)
    twist_forward(sums_ref, cos_ref, sin_ref, z_ref, 8)
    rows_of(z_ref, fr_ref, filt_ref, 8)
    taps_ref[...] = jnp.zeros_like(taps_ref)

    def group(g, carry):
        data = jnp.concatenate(
            [in_ref[:, g, n * 16 : n * 16 + 16, :].reshape(A * 16, L) for n in range(4)], axis=1
        )
        sums_ref[...] = mm(fp_ref[...], data)
        twist_forward(sums_ref, cos_ref, sin_ref, z_ref, 16)
        rows_of(z_ref, fr_ref, spec_ref, 16)
        for k in range(KH):
            for n in range(4):
                re = slice(n * 256, n * 256 + L)
                im = slice(n * 256 + L, n * 256 + 256)
                r8 = slice(k * 8, k * 8 + 8)
                rg = slice(k * 16, k * 16 + 8)
                rr = slice(k * 16 + 8, k * 16 + 16)
                fr, fi = filt_ref[r8, re], filt_ref[r8, im]
                gr, gi = spec_ref[rg, re], spec_ref[rg, im]
                hr, hi = spec_ref[rr, re], spec_ref[rr, im]
                taps_ref[r8, re] += hr * gr + hi * gi
                taps_ref[r8, im] += hi * gr - hr * gi
                rows = slice(k * 16, k * 16 + 16)
                y_ref[rows, re] = jnp.concatenate(
                    [gr * fr - gi * fi, hr * fr + hi * fi], axis=0
                ).astype(BF)
                y_ref[rows, im] = jnp.concatenate(
                    [gr * fi + gi * fr, hi * fr - hr * fi], axis=0
                ).astype(BF)
        rows_of(y_ref, ir_ref, spec_ref, 16)
        twist_back(spec_ref, cos_ref, sin_ref, u_ref, 16)
        result = mm(ip_ref[...], u_ref[...])
        for n in range(4):
            out_ref[:, g, n * 16 : n * 16 + 16, :] = (
                result[:, n * L : (n + 1) * L].astype(BF).reshape(A, 16, L)
            )
        return carry

    lax.fori_loop(0, X, group, 0)

    y_ref[: KH * 8, :] = taps_ref[...].astype(BF)
    rows_of(y_ref, ir_ref, spec_ref, 8)
    twist_back(spec_ref, cos_ref, sin_ref, u_ref, 8)
    result = mm(io_ref[...], u_ref[: 2 * A * 8, :])
    place = lax.broadcasted_iota(jnp.int32, (A * 8, L), 0) % 8 // 2
    for g in range(4):
        total = jnp.zeros((A * 8, L), F32)
        for n in range(4):
            moved = pltpu.roll(result[:, n * L : (n + 1) * L], (2 * (n - g)) % (A * 8), 0)
            total = jnp.where(place == n, moved, total)
        out_ref[:, g, 64:72, :] = total.reshape(A, 8, L).astype(BF)


def transform(fields, t):
    pair = KH * 16
    return pl.pallas_call(
        transform_kernel,
        out_shape=jax.ShapeDtypeStruct((A, X, ROWS, L), BF),
        in_specs=[whole()] * 9,
        out_specs=whole(),
        scratch_shapes=[
            pltpu.VMEM((2 * pair, SEG), F32),
            pltpu.VMEM((pair, 2 * SEG), BF),
            pltpu.VMEM((pair, 2 * SEG), F32),
            pltpu.VMEM((pair, 2 * SEG), BF),
            pltpu.VMEM((2 * A * 16, SEG), BF),
            pltpu.VMEM((KH * 8, 2 * SEG), F32),
            pltpu.VMEM((KH * 8, 2 * SEG), F32),
        ],
        compiler_params=pltpu.CompilerParams(vmem_limit_bytes=48 * MIB),
        name="transform",
    )(
        fields, t["fwd_pair"], t["fwd_one"], t["inv_pair"], t["inv_one"],
        t["fwd_rows"], t["inv_rows"], t["cos_twist"], t["sin_twist"],
    )


def finish_kernel(
    in_ref, q_ref, k_ref, v_ref, o_ref, skip_ref, order_ref, dq_ref, dk_ref, dv_ref, df_ref
):
    step = pl.program_id(0)

    def in_place(rows):
        return lax.dot_general(
            rows.astype(BF), order_ref[...], (((0,), (0,)), ((), ())), preferred_element_type=F32
        )

    for half in range(2):
        part = up(
            in_ref[half * 64 : half * 64 + 64, pl.ds(pl.multiple_of(step * 16, 16), 16), :]
        )
        rows = jnp.concatenate(
            [part[:, :8].reshape(512, L), part[:, 8:].reshape(512, L)], axis=1
        )
        conv = in_place(rows)
        for g in range(4):
            cols = slice(g * 256 + half * 128, g * 256 + half * 128 + 128)
            state = conv[:L, g * L : (g + 1) * L]
            back = conv[L:, g * L : (g + 1) * L]
            q, k, v, o = (up(ref[:, cols]) for ref in (q_ref, k_ref, v_ref, o_ref))
            skip = skip_ref[:, cols]
            mixed = state + skip * up((k * v).astype(BF))
            total = back + skip * up((q * o).astype(BF))
            dq_ref[:, cols] = (o * mixed).astype(BF)
            dk_ref[:, cols] = (total * v).astype(BF)
            dv_ref[:, cols] = (total * k).astype(BF)

    @pl.when(step == 0)
    def _():
        for half in range(2):
            rows = up(in_ref[half * 64 : half * 64 + 64, 64:72, :]).reshape(512, L)
            taps = in_place(rows)
            for n in range(4):
                df_ref[n * L : (n + 1) * L, half * 128 : half * 128 + 128] = taps[
                    :, n * L : (n + 1) * L
                ]


def finish(fields, q_in, k_in, v_in, out_grad, skip, order):
    field = pl.BlockSpec((L, 1024), lambda i: (i, 0))
    return pl.pallas_call(
        finish_kernel,
        out_shape=(
            jax.ShapeDtypeStruct((SEG, 1024), BF),
            jax.ShapeDtypeStruct((SEG, 1024), BF),
            jax.ShapeDtypeStruct((SEG, 1024), BF),
            jax.ShapeDtypeStruct((SEG, 256), F32),
        ),
        grid=(4,),
        in_specs=[pl.BlockSpec((DEV, ROWS, L), lambda i: (0, 0, 0))]
        + [field] * 4
        + [
            pl.BlockSpec((1, 1024), lambda i: (0, 0)),
            pl.BlockSpec((512, 512), lambda i: (0, 0)),
        ],
        out_specs=(field, field, field, pl.BlockSpec((SEG, 256), lambda i: (0, 0))),
        compiler_params=pltpu.CompilerParams(vmem_limit_bytes=40 * MIB),
        name="finish",
    )(fields, q_in, k_in, v_in, out_grad, skip, order)


def body(q_in, k_in, v_in, out_grad, filters, skip):
    t = {name: jnp.asarray(value) for name, value in constants().items()}
    index = lax.axis_index("ch").astype(jnp.int32).reshape(1)
    sent = pack(index, q_in, k_in, v_in, out_grad, filters, t["order"])
    columns = lax.all_to_all(sent, ("ctx", "ch"), split_axis=0, concat_axis=0, tiled=True)
    results = transform(columns.reshape(A, X, ROWS, L), t)
    blocks = lax.all_to_all(
        results.reshape(DEV, ROWS, L), ("ctx", "ch"), split_axis=0, concat_axis=0, tiled=True
    )
    return finish(blocks, q_in, k_in, v_in, out_grad, skip.reshape(1, 1024), t["order"])


def solution(mesh):
    return jax.shard_map(
        body,
        mesh=mesh,
        in_specs=(
            P("ctx", "ch"),
            P("ctx", "ch"),
            P("ctx", "ch"),
            P("ctx", "ch"),
            P("ctx", None),
            P("ch"),
        ),
        out_specs=(P("ctx", "ch"), P("ctx", "ch"), P("ctx", "ch"), P("ctx", "ch")),
        check_vma=False,
    )
```

```python
import functools
import math

import jax
import jax.numpy as jnp
import ml_dtypes
import numpy as np
from jax import lax
from jax.experimental import pallas as pl
from jax.experimental.pallas import tpu as pltpu
from jax.sharding import PartitionSpec as P

BF = jnp.bfloat16
F32 = jnp.float32

A = 32
X = 4
DEV = A * X
L = 128
SEG = 4 * L
KH = A + 1
PERIOD = 2 * A * SEG
ROWS = 72
MIB = 1024 * 1024


def low(table):
    return np.asarray(table, np.float32).astype(ml_dtypes.bfloat16)


def spread(table, count):
    return np.kron(table, np.eye(count))


@functools.cache
def constants():
    k = np.arange(KH)[:, None]
    a = np.arange(A)[None, :]
    angle = 2 * np.pi * (k * a % (2 * A)) / (2 * A)
    cos_block = low(np.cos(angle)).astype(np.float64)
    sin_block = low(np.sin(angle)).astype(np.float64)
    cos_block[np.abs(cos_block) < 1e-6] = 0.0
    sin_block[np.abs(sin_block) < 1e-6] = 0.0
    forward = np.concatenate([cos_block, -sin_block], 0)
    weight = np.where((k == 0) | (k == A), 1.0, 2.0) / PERIOD
    backward = np.concatenate([weight * cos_block, -(weight * sin_block)[1:A]], 0).T
    l = np.arange(L)[:, None]
    fwd_rows, inv_rows = [], []
    for r in range(4):
        q = r + 4 * np.arange(L)[None, :]
        angle = 2 * np.pi * (l * q % SEG) / SEG
        c, s = np.cos(angle), np.sin(angle)
        fwd_rows.append(np.block([[c, -s], [s, c]]))
        inv_rows.append(np.block([[c.T, s.T], [-s.T, c.T]]))
    j = np.arange(SEG)[None, :]
    twist = 2 * np.pi * (k * j % PERIOD) / PERIOD
    row = np.arange(512)
    column = (row // 2) % 4 * 128 + row // 8 * 2 + row % 2
    order = np.zeros((512, 512))
    order[row, column] = 1.0
    return {
        "forward": low(spread(forward, 8)),
        "backward": low(spread(backward, 8)),
        "fwd_rows": low(np.stack(fwd_rows)),
        "inv_rows": low(np.stack(inv_rows)),
        "cos_twist": np.cos(twist).astype(np.float32),
        "sin_twist": np.sin(twist).astype(np.float32),
        "order": low(order),
    }


def mm(left, right):
    return jnp.dot(left, right, preferred_element_type=F32)


def up(value):
    return value.astype(F32)


def whole():
    return pl.BlockSpec(memory_space=pltpu.VMEM)


def pack_kernel(
    index_ref, q_hbm, k_hbm, v_hbm, o_hbm, f_hbm, order_hbm, out_ref,
    fields_ref, taps_ref, order_ref, field_sems, other_sems,
):
    step = pl.program_id(0)
    sources = (k_hbm, v_hbm, q_hbm, o_hbm)

    def field_copy(i, n):
        rows = pl.ds(pl.multiple_of(n * L, L), L)
        return pltpu.make_async_copy(
            sources[i].at[rows], fields_ref.at[i, rows], field_sems.at[n, i]
        )

    def taps_copy():
        rows = pl.ds(pl.multiple_of(index_ref[0] * L, L), L)
        return pltpu.make_async_copy(f_hbm.at[rows], taps_ref, other_sems.at[0])

    def order_copy():
        return pltpu.make_async_copy(order_hbm, order_ref, other_sems.at[1])

    @pl.when(step == 0)
    def _():
        for i in range(4):
            field_copy(i, 0).start()
        order_copy().start()
        for n in range(1, 4):
            for i in range(4):
                field_copy(i, n).start()
        taps_copy().start()
        order_copy().wait()

    def by_owner(field, half):
        columns = jnp.concatenate(
            [field[:, g * 256 + half * 128 : g * 256 + half * 128 + 128] for g in range(4)], axis=1
        )
        return lax.dot_general(
            order_ref[...], columns, (((1,), (1,)), ((), ())), preferred_element_type=F32
        )

    @pl.when(step < 4)
    def _():
        for i in range(4):
            field_copy(i, step).wait()
        rows = pl.ds(pl.multiple_of(step * L, L), L)
        k, v, q, o = (up(fields_ref[i, rows, :]) for i in range(4))
        both = jnp.concatenate([(k * v).astype(BF), (q * o).astype(BF)], axis=0)
        for half in range(2):
            moved = by_owner(both, half)
            pair = jnp.concatenate(
                [moved[:, :L].reshape(64, 8, L), moved[:, L:].reshape(64, 8, L)], axis=1
            )
            out_ref[half * 64 : half * 64 + 64, :, :] = pair.astype(BF)

    @pl.when(step == 4)
    def _():
        taps_copy().wait()
        taps = taps_ref[...].astype(BF)
        for half in range(2):
            moved = by_owner(taps, half).reshape(64, 8, L)
            out_ref[half * 64 : half * 64 + 64, :8, :] = moved.astype(BF)


def pack(index, q_in, k_in, v_in, out_grad, filters, order):
    return pl.pallas_call(
        pack_kernel,
        out_shape=jax.ShapeDtypeStruct((DEV, ROWS, L), BF),
        grid_spec=pltpu.PrefetchScalarGridSpec(
            num_scalar_prefetch=1,
            grid=(5,),
            in_specs=[pl.BlockSpec(memory_space=pl.ANY)] * 6,
            out_specs=pl.BlockSpec((DEV, 16, L), lambda i, s: (0, i, 0)),
            scratch_shapes=[
                pltpu.VMEM((4, SEG, 1024), BF),
                pltpu.VMEM((L, 1024), F32),
                pltpu.VMEM((512, 512), BF),
                pltpu.SemaphoreType.DMA((4, 4)),
                pltpu.SemaphoreType.DMA((2,)),
            ],
        ),
        compiler_params=pltpu.CompilerParams(vmem_limit_bytes=60 * MIB),
        name="pack",
    )(index, q_in, k_in, v_in, out_grad, filters, order)


def quarters(value):
    return [value[:, i * L : (i + 1) * L] for i in range(4)]


def butterfly(re, im, sign):
    ar, br, cr, dr = re[0] + re[2], re[0] - re[2], re[1] + re[3], re[1] - re[3]
    ai, bi, ci, di = im[0] + im[2], im[0] - im[2], im[1] + im[3], im[1] - im[3]
    plus = (br - di, bi + dr)
    minus = (br + di, bi - dr)
    first, third = (plus, minus) if sign > 0 else (minus, plus)
    return [(ar + cr, ai + ci), first, (ar - cr, ai - ci), third]


def twist_forward(fields, cos_ref, sin_ref, k):
    c = cos_ref[k : k + 1, :]
    s = sin_ref[k : k + 1, :]
    found = []
    for sums_ref in fields:
        re = sums_ref[k * 8 : k * 8 + 8, :]
        im = sums_ref[(KH + k) * 8 : (KH + k) * 8 + 8, :]
        parts = butterfly(quarters(re * c + im * s), quarters(im * c - re * s), -1)
        found.append(jnp.concatenate([part for pair in parts for part in pair], axis=1))
    return found


def store_rows(ref, row, pieces):
    ref[row : row + 8 * len(pieces), :] = jnp.concatenate(pieces, axis=0).astype(BF)


def twist_back(rows_ref, cos_ref, sin_ref, row, k):
    re = [rows_ref[row : row + 8, n * 256 : n * 256 + L] for n in range(4)]
    im = [rows_ref[row : row + 8, n * 256 + L : n * 256 + 256] for n in range(4)]
    real, imag = [], []
    for n, (ur, ui) in enumerate(butterfly(re, im, 1)):
        c = cos_ref[k : k + 1, n * L : (n + 1) * L]
        s = sin_ref[k : k + 1, n * L : (n + 1) * L]
        real.append(ur * c - ui * s)
        imag.append(ui * c + ur * s)
    return jnp.concatenate(real, axis=1), jnp.concatenate(imag, axis=1)


def interleave(first, second):
    n, m = len(first), len(second)
    if n == 0 or m == 0:
        order = list(first) + list(second)
    else:
        order = []
        done = 0
        for i, piece in enumerate(first):
            order.append(piece)
            upto = (i + 1) * m // n
            order.extend(second[done:upto])
            done = upto
    for piece in order:
        piece()


PAIRS = [(0, 1, A)] + [(k, k + 1) for k in range(2, A, 2)]


def transform_kernel(
    in_ref, fwd_ref, inv_ref, fr_ref, ir_ref, cos_ref, sin_ref, out_ref,
    sums_ref, z_ref, spec_ref, y_ref, v_ref, u_ref, filt_sums, filt_z, filt_ref, taps_ref,
):
    def load(g, n, field):
        rows = up(in_ref[:, g, n * 16 : n * 16 + 16, :])
        return rows[:, field * 8 : field * 8 + 8].reshape(A * 8, L).astype(BF)

    def block_sums(g):
        def piece(field, half):
            data = jnp.concatenate([load(g, 2 * half + i, field) for i in range(2)], axis=1)
            sums_ref[g % 2, field, :, half * 256 : half * 256 + 256] = mm(fwd_ref[...], data)

        return [lambda f=f, h=h: piece(f, h) for f in range(2) for h in range(2)]

    def forward_twist(g):
        def piece(k):
            fields = [sums_ref.at[g % 2, 0], sums_ref.at[g % 2, 1]]
            store_rows(z_ref.at[g % 2], k * 16, twist_forward(fields, cos_ref, sin_ref, k))

        return [lambda k=k: piece(k) for k in range(KH)]

    def row_sums(data, table, out):
        def piece(n):
            cols = slice(n * 256, (n + 1) * 256)
            out[:, cols] = mm(data[:, cols], table[n])

        return [lambda n=n: piece(n) for n in range(4)]

    def products(g):
        def piece(k):
            spec, y = spec_ref.at[g % 2], y_ref.at[g % 2]
            r8 = slice(k * 8, k * 8 + 8)
            rg = slice(k * 16, k * 16 + 8)
            rr = slice(k * 16 + 8, k * 16 + 16)
            for n in range(4):
                re = slice(n * 256, n * 256 + L)
                im = slice(n * 256 + L, n * 256 + 256)
                fr, fi = filt_ref[r8, re], filt_ref[r8, im]
                gr, gi = spec[rg, re], spec[rg, im]
                hr, hi = spec[rr, re], spec[rr, im]
                wr = hr * gr + hi * gi
                wi = hi * gr - hr * gi
                if g > 0:
                    wr = wr + taps_ref[r8, re]
                    wi = wi + taps_ref[r8, im]
                taps_ref[r8, re] = wr
                taps_ref[r8, im] = wi
                rows = slice(k * 16, k * 16 + 16)
                y[rows, re] = jnp.concatenate(
                    [gr * fr - gi * fi, hr * fr + hi * fi], axis=0
                ).astype(BF)
                y[rows, im] = jnp.concatenate(
                    [gr * fi + gi * fr, hi * fr - hr * fi], axis=0
                ).astype(BF)

        return [lambda k=k: piece(k) for k in range(KH)]

    def back_twist(rows, place, out):
        def piece(ks):
            parts = [twist_back(rows, cos_ref, sin_ref, place(k), k) for k in ks]
            store_rows(out, ks[0] * 8, [parts[0][0], parts[1][0]])
            if len(ks) == 3:
                store_rows(out, A * 8, [parts[2][0], parts[1][1]])
            else:
                store_rows(out, (A + ks[0]) * 8, [parts[0][1], parts[1][1]])

        return [lambda ks=ks: piece(ks) for ks in PAIRS]

    def results(g):
        def piece(half):
            cols = slice(half * 256, half * 256 + 256)
            state = mm(inv_ref[...], u_ref[g % 2, 0, :, cols]).reshape(A, 8, 256)
            back = mm(inv_ref[...], u_ref[g % 2, 1, :, cols]).reshape(A, 8, 256)
            both = jnp.concatenate([state, back], axis=1).astype(BF)
            for i in range(2):
                n = 2 * half + i
                out_ref[:, g, n * 16 : n * 16 + 16, :] = both[:, :, i * L : (i + 1) * L]

        return [lambda h=h: piece(h) for h in range(2)]

    def forward_rows(g):
        return row_sums(z_ref.at[g % 2], fr_ref, spec_ref.at[g % 2])

    def back_rows(g):
        return row_sums(y_ref.at[g % 2], ir_ref, v_ref.at[g % 2])

    def back_twists(g):
        pieces = []
        for f in range(2):
            pieces += back_twist(
                v_ref.at[g % 2], lambda k, f=f: k * 16 + f * 8, u_ref.at[g % 2, f]
            )
        return pieces

    def filter_sums():
        def piece(half):
            data = jnp.concatenate(
                [
                    up(in_ref[:, 2 * half + i, 64:72, :]).reshape(A * 8, L).astype(BF)
                    for i in range(2)
                ],
                axis=1,
            )
            filt_sums[:, half * 256 : half * 256 + 256] = mm(fwd_ref[...], data)

        return [lambda h=h: piece(h) for h in range(2)]

    def filter_twist():
        def piece(ks):
            found = [twist_forward([filt_sums], cos_ref, sin_ref, k)[0] for k in ks]
            store_rows(filt_z, ks[0] * 8, found)

        return [lambda ks=ks: piece(ks) for ks in [(k, k + 1) for k in range(0, A, 2)] + [(A,)]]

    def taps_rows():
        def piece(k):
            filt_z[k * 8 : k * 8 + 16, :] = taps_ref[k * 8 : k * 8 + 16, :].astype(BF)

        def last():
            filt_z[A * 8 :, :] = taps_ref[A * 8 :, :].astype(BF)

        return [lambda k=k: piece(k) for k in range(0, A, 2)] + [last]

    interleave(filter_sums() + block_sums(0), [])
    interleave(block_sums(1)[:2], filter_twist())
    interleave(row_sums(filt_z, fr_ref, filt_ref) + block_sums(1)[2:], forward_twist(0))
    for g in range(X):
        interleave(forward_rows(g), back_twists(g - 1) if g > 0 else [])
        interleave(results(g - 1) if g > 0 else [], products(g))
        interleave(back_rows(g), forward_twist(g + 1) if g + 1 < X else taps_rows())
        if g + 2 < X:
            interleave(block_sums(g + 2), [])
    interleave(row_sums(filt_z, ir_ref, filt_ref), back_twists(X - 1))
    interleave(results(X - 1), back_twist(filt_ref, lambda k: k * 8, u_ref.at[0, 0]))

    result = mm(inv_ref[...], u_ref[0, 0]) * (1.0 / 256.0)
    place = lax.broadcasted_iota(jnp.int32, (A * 8, L), 0) % 8 // 2
    for g in range(4):
        total = result[:, :L] if g == 0 else pltpu.roll(result[:, :L], (-2 * g) % (A * 8), 0)
        for n in range(1, 4):
            part = result[:, n * L : (n + 1) * L]
            moved = part if n == g else pltpu.roll(part, (2 * (n - g)) % (A * 8), 0)
            total = jnp.where(place == n, moved, total)
        out_ref[:, g, 64:72, :] = total.reshape(A, 8, L).astype(BF)


def transform(fields, t):
    return pl.pallas_call(
        transform_kernel,
        out_shape=jax.ShapeDtypeStruct((A, X, ROWS, L), BF),
        in_specs=[whole()] * 7,
        out_specs=whole(),
        scratch_shapes=[
            pltpu.VMEM((2, 2, 2 * KH * 8, SEG), F32),
            pltpu.VMEM((2, KH * 16, 2 * SEG), BF),
            pltpu.VMEM((2, KH * 16, 2 * SEG), F32),
            pltpu.VMEM((2, KH * 16, 2 * SEG), BF),
            pltpu.VMEM((2, KH * 16, 2 * SEG), F32),
            pltpu.VMEM((2, 2, 2 * A * 8, SEG), BF),
            pltpu.VMEM((2 * KH * 8, SEG), F32),
            pltpu.VMEM((KH * 8, 2 * SEG), BF),
            pltpu.VMEM((KH * 8, 2 * SEG), F32),
            pltpu.VMEM((KH * 8, 2 * SEG), F32),
        ],
        compiler_params=pltpu.CompilerParams(vmem_limit_bytes=36 * MIB),
        name="transform",
    )(
        fields, t["forward"], t["backward"], t["fwd_rows"], t["inv_rows"],
        t["cos_twist"], t["sin_twist"],
    )


def finish_kernel(
    in_ref, q_ref, k_ref, v_ref, o_ref, skip_ref, order_ref, dq_ref, dk_ref, dv_ref, df_ref
):
    step = pl.program_id(0)

    def in_place(rows):
        return lax.dot_general(
            rows.astype(BF), order_ref[...], (((0,), (0,)), ((), ())), preferred_element_type=F32
        )

    for half in range(2):
        part = up(
            in_ref[half * 64 : half * 64 + 64, pl.ds(pl.multiple_of(step * 16, 16), 16), :]
        )
        rows = jnp.concatenate(
            [part[:, :8].reshape(512, L), part[:, 8:].reshape(512, L)], axis=1
        )
        conv = in_place(rows)
        for g in range(4):
            cols = slice(g * 256 + half * 128, g * 256 + half * 128 + 128)
            state = conv[:L, g * L : (g + 1) * L]
            back = conv[L:, g * L : (g + 1) * L]
            q, k, v, o = (up(ref[:, cols]) for ref in (q_ref, k_ref, v_ref, o_ref))
            skip = skip_ref[:, cols]
            mixed = state + skip * up((k * v).astype(BF))
            total = back + skip * up((q * o).astype(BF))
            dq_ref[:, cols] = (o * mixed).astype(BF)
            dk_ref[:, cols] = (total * v).astype(BF)
            dv_ref[:, cols] = (total * k).astype(BF)

    @pl.when(step == 0)
    def _():
        for half in range(2):
            rows = up(in_ref[half * 64 : half * 64 + 64, 64:72, :]).reshape(512, L)
            taps = in_place(rows)
            for n in range(4):
                df_ref[n * L : (n + 1) * L, half * 128 : half * 128 + 128] = taps[
                    :, n * L : (n + 1) * L
                ]


def finish(fields, q_in, k_in, v_in, out_grad, skip, order):
    field = pl.BlockSpec((L, 1024), lambda i: (i, 0))
    return pl.pallas_call(
        finish_kernel,
        out_shape=(
            jax.ShapeDtypeStruct((SEG, 1024), BF),
            jax.ShapeDtypeStruct((SEG, 1024), BF),
            jax.ShapeDtypeStruct((SEG, 1024), BF),
            jax.ShapeDtypeStruct((SEG, 256), F32),
        ),
        grid=(4,),
        in_specs=[pl.BlockSpec((DEV, ROWS, L), lambda i: (0, 0, 0))]
        + [field] * 4
        + [
            pl.BlockSpec((1, 1024), lambda i: (0, 0)),
            pl.BlockSpec((512, 512), lambda i: (0, 0)),
        ],
        out_specs=(field, field, field, pl.BlockSpec((SEG, 256), lambda i: (0, 0))),
        compiler_params=pltpu.CompilerParams(vmem_limit_bytes=40 * MIB),
        name="finish",
    )(fields, q_in, k_in, v_in, out_grad, skip, order)


def body(q_in, k_in, v_in, out_grad, filters, skip):
    t = {name: jnp.asarray(value) for name, value in constants().items()}
    index = lax.axis_index("ch").astype(jnp.int32).reshape(1)
    sent = pack(index, q_in, k_in, v_in, out_grad, filters, t["order"])
    columns = lax.all_to_all(sent, ("ctx", "ch"), split_axis=0, concat_axis=0, tiled=True)
    results = transform(columns.reshape(A, X, ROWS, L), t)
    blocks = lax.all_to_all(
        results.reshape(DEV, ROWS, L), ("ctx", "ch"), split_axis=0, concat_axis=0, tiled=True
    )
    return finish(blocks, q_in, k_in, v_in, out_grad, skip.reshape(1, 1024), t["order"])


def solution(mesh):
    return jax.shard_map(
        body,
        mesh=mesh,
        in_specs=(
            P("ctx", "ch"),
            P("ctx", "ch"),
            P("ctx", "ch"),
            P("ctx", "ch"),
            P("ctx", None),
            P("ch"),
        ),
        out_specs=(P("ctx", "ch"), P("ctx", "ch"), P("ctx", "ch"), P("ctx", "ch")),
        check_vma=False,
    )
```

```python
import functools
import math

import jax
import jax.numpy as jnp
import ml_dtypes
import numpy as np
from jax import lax
from jax.experimental import pallas as pl
from jax.experimental.pallas import tpu as pltpu
from jax.sharding import PartitionSpec as P

BF = jnp.bfloat16
F32 = jnp.float32

A = 32
X = 4
DEV = A * X
L = 128
SEG = 4 * L
KH = A + 1
PERIOD = 2 * A * SEG
ROWS = 72
MIB = 1024 * 1024


def low(table):
    return np.asarray(table, np.float32).astype(ml_dtypes.bfloat16)


def spread(table, count):
    return np.kron(table, np.eye(count))


@functools.cache
def constants():
    k = np.arange(KH)[:, None]
    a = np.arange(A)[None, :]
    angle = 2 * np.pi * (k * a % (2 * A)) / (2 * A)
    cos_block = low(np.cos(angle)).astype(np.float64)
    sin_block = low(np.sin(angle)).astype(np.float64)
    cos_block[np.abs(cos_block) < 1e-6] = 0.0
    sin_block[np.abs(sin_block) < 1e-6] = 0.0
    forward = np.concatenate([cos_block, -sin_block], 0)
    weight = np.where((k == 0) | (k == A), 1.0, 2.0) / PERIOD
    backward = np.concatenate([weight * cos_block, -(weight * sin_block)[1:A]], 0).T
    l = np.arange(L)[:, None]
    fwd_rows, inv_rows = [], []
    for r in range(4):
        q = r + 4 * np.arange(L)[None, :]
        angle = 2 * np.pi * (l * q % SEG) / SEG
        c, s = np.cos(angle), np.sin(angle)
        fwd_rows.append(np.block([[c, -s], [s, c]]))
        inv_rows.append(np.block([[c.T, s.T], [-s.T, c.T]]))
    j = np.arange(SEG)[None, :]
    twist = 2 * np.pi * (k * j % PERIOD) / PERIOD
    row = np.arange(512)
    column = (row // 2) % 4 * 128 + row // 8 * 2 + row % 2
    order = np.zeros((512, 512))
    order[row, column] = 1.0
    return {
        "forward": low(spread(forward, 8)),
        "backward": low(spread(backward, 8)),
        "fwd_rows": low(np.stack(fwd_rows)),
        "inv_rows": low(np.stack(inv_rows)),
        "cos_twist": np.cos(twist).astype(np.float32),
        "sin_twist": np.sin(twist).astype(np.float32),
        "order": low(order),
    }


def mm(left, right):
    return jnp.dot(left, right, preferred_element_type=F32)


def up(value):
    return value.astype(F32)


def whole():
    return pl.BlockSpec(memory_space=pltpu.VMEM)


def pack_kernel(
    q_hbm, k_hbm, v_hbm, o_hbm, f_hbm, out_hbm,
    fields_ref, taps_ref, order_ref, pair_ref, tail_ref, field_sems, taps_sem, out_sems,
):
    sources = (k_hbm, v_hbm, q_hbm, o_hbm)

    def field_copy(i, n):
        rows = pl.ds(n * L, L)
        return pltpu.make_async_copy(
            sources[i].at[rows], fields_ref.at[i, rows], field_sems.at[n, i]
        )

    rows = pl.ds(pl.multiple_of(lax.axis_index("ch") * L, L), L)
    taps_copy = pltpu.make_async_copy(f_hbm.at[rows], taps_ref, taps_sem)
    for n in range(4):
        for i in range(4):
            field_copy(i, n).start()
    taps_copy.start()
    row = lax.broadcasted_iota(jnp.int32, (512, 512), 0)
    column = lax.broadcasted_iota(jnp.int32, (512, 512), 1)
    source = row // 2 % 4 * 128 + row // 8 * 2 + row % 2
    order_ref[...] = jnp.where(column == source, 1.0, 0.0).astype(BF)

    def by_owner(field, half):
        columns = jnp.concatenate(
            [field[:, g * 256 + half * 128 : g * 256 + half * 128 + 128] for g in range(4)], axis=1
        )
        return lax.dot_general(
            order_ref[...], columns, (((1,), (1,)), ((), ())), preferred_element_type=F32
        )

    copies = []
    for n in range(4):
        for i in range(4):
            field_copy(i, n).wait()
        k, v, q, o = (up(fields_ref[i, n * L : (n + 1) * L, :]) for i in range(4))
        both = jnp.concatenate([(k * v).astype(BF), (q * o).astype(BF)], axis=0)
        for half in range(2):
            moved = by_owner(both, half)
            pair = jnp.concatenate(
                [moved[:, :L].reshape(64, 8, L), moved[:, L:].reshape(64, 8, L)], axis=1
            )
            pair_ref[n, half * 64 : half * 64 + 64, :, :] = pair.astype(BF)
        copies.append(
            pltpu.make_async_copy(
                pair_ref.at[n], out_hbm.at[:, pl.ds(n * 16, 16), :], out_sems.at[n]
            )
        )
        copies[-1].start()
    taps_copy.wait()
    taps = taps_ref[...].astype(BF)
    for half in range(2):
        moved = by_owner(taps, half).reshape(64, 8, L)
        tail_ref[half * 64 : half * 64 + 64, :, :] = moved.astype(BF)
    copies.append(
        pltpu.make_async_copy(tail_ref, out_hbm.at[:, pl.ds(64, 8), :], out_sems.at[4])
    )
    copies[-1].start()
    for copy in copies:
        copy.wait()


def pack(q_in, k_in, v_in, out_grad, filters):
    return pl.pallas_call(
        pack_kernel,
        out_shape=jax.ShapeDtypeStruct((DEV, ROWS, L), BF),
        in_specs=[pl.BlockSpec(memory_space=pl.ANY)] * 5,
        out_specs=pl.BlockSpec(memory_space=pl.ANY),
        scratch_shapes=[
            pltpu.VMEM((4, SEG, 1024), BF),
            pltpu.VMEM((L, 1024), F32),
            pltpu.VMEM((512, 512), BF),
            pltpu.VMEM((4, DEV, 16, L), BF),
            pltpu.VMEM((DEV, 8, L), BF),
            pltpu.SemaphoreType.DMA((4, 4)),
            pltpu.SemaphoreType.DMA,
            pltpu.SemaphoreType.DMA((5,)),
        ],
        compiler_params=pltpu.CompilerParams(vmem_limit_bytes=60 * MIB),
        name="pack",
    )(q_in, k_in, v_in, out_grad, filters)


def quarters(value):
    return [value[:, i * L : (i + 1) * L] for i in range(4)]


def butterfly(re, im, sign):
    ar, br, cr, dr = re[0] + re[2], re[0] - re[2], re[1] + re[3], re[1] - re[3]
    ai, bi, ci, di = im[0] + im[2], im[0] - im[2], im[1] + im[3], im[1] - im[3]
    plus = (br - di, bi + dr)
    minus = (br + di, bi - dr)
    first, third = (plus, minus) if sign > 0 else (minus, plus)
    return [(ar + cr, ai + ci), first, (ar - cr, ai - ci), third]


def twist_forward(fields, cos_ref, sin_ref, k):
    c = cos_ref[k : k + 1, :]
    s = sin_ref[k : k + 1, :]
    found = []
    for sums_ref in fields:
        re = sums_ref[k * 8 : k * 8 + 8, :]
        im = sums_ref[(KH + k) * 8 : (KH + k) * 8 + 8, :]
        parts = butterfly(quarters(re * c + im * s), quarters(im * c - re * s), -1)
        found.append(jnp.concatenate([part for pair in parts for part in pair], axis=1))
    return found


def store_rows(ref, row, pieces):
    ref[row : row + 8 * len(pieces), :] = jnp.concatenate(pieces, axis=0).astype(BF)


def twist_back(rows_ref, cos_ref, sin_ref, row, k):
    re = [rows_ref[row : row + 8, n * 256 : n * 256 + L] for n in range(4)]
    im = [rows_ref[row : row + 8, n * 256 + L : n * 256 + 256] for n in range(4)]
    real, imag = [], []
    for n, (ur, ui) in enumerate(butterfly(re, im, 1)):
        c = cos_ref[k : k + 1, n * L : (n + 1) * L]
        s = sin_ref[k : k + 1, n * L : (n + 1) * L]
        real.append(ur * c - ui * s)
        imag.append(ui * c + ur * s)
    return jnp.concatenate(real, axis=1), jnp.concatenate(imag, axis=1)


def interleave(first, second):
    n, m = len(first), len(second)
    if n == 0 or m == 0:
        order = list(first) + list(second)
    else:
        order = []
        done = 0
        for i, piece in enumerate(first):
            order.append(piece)
            upto = (i + 1) * m // n
            order.extend(second[done:upto])
            done = upto
    for piece in order:
        piece()


PAIRS = [(0, 1, A)] + [(k, k + 1) for k in range(2, A, 2)]


def transform_kernel(
    in_ref, fwd_ref, inv_ref, fr_ref, ir_ref, cos_ref, sin_ref, out_ref,
    sums_ref, z_ref, spec_ref, y_ref, v_ref, u_ref, filt_sums, filt_z, filt_ref, taps_ref,
):
    def load(g, n, field):
        rows = up(in_ref[:, g, n * 16 : n * 16 + 16, :])
        return rows[:, field * 8 : field * 8 + 8].reshape(A * 8, L).astype(BF)

    def block_sums(g):
        def piece(field, half):
            data = jnp.concatenate([load(g, 2 * half + i, field) for i in range(2)], axis=1)
            sums_ref[g % 2, field, :, half * 256 : half * 256 + 256] = mm(fwd_ref[...], data)

        return [lambda f=f, h=h: piece(f, h) for f in range(2) for h in range(2)]

    def forward_twist(g):
        def piece(k):
            fields = [sums_ref.at[g % 2, 0], sums_ref.at[g % 2, 1]]
            store_rows(z_ref.at[g % 2], k * 16, twist_forward(fields, cos_ref, sin_ref, k))

        return [lambda k=k: piece(k) for k in range(KH)]

    def row_sums(data, table, out):
        def piece(n):
            cols = slice(n * 256, (n + 1) * 256)
            out[:, cols] = mm(data[:, cols], table[n])

        return [lambda n=n: piece(n) for n in range(4)]

    def products(g):
        def piece(k):
            spec, y = spec_ref.at[g % 2], y_ref.at[g % 2]
            r8 = slice(k * 8, k * 8 + 8)
            rg = slice(k * 16, k * 16 + 8)
            rr = slice(k * 16 + 8, k * 16 + 16)
            for n in range(4):
                re = slice(n * 256, n * 256 + L)
                im = slice(n * 256 + L, n * 256 + 256)
                fr, fi = filt_ref[r8, re], filt_ref[r8, im]
                gr, gi = spec[rg, re], spec[rg, im]
                hr, hi = spec[rr, re], spec[rr, im]
                wr = hr * gr + hi * gi
                wi = hi * gr - hr * gi
                if g > 0:
                    wr = wr + taps_ref[r8, re]
                    wi = wi + taps_ref[r8, im]
                taps_ref[r8, re] = wr
                taps_ref[r8, im] = wi
                rows = slice(k * 16, k * 16 + 16)
                y[rows, re] = jnp.concatenate(
                    [gr * fr - gi * fi, hr * fr + hi * fi], axis=0
                ).astype(BF)
                y[rows, im] = jnp.concatenate(
                    [gr * fi + gi * fr, hi * fr - hr * fi], axis=0
                ).astype(BF)

        return [lambda k=k: piece(k) for k in range(KH)]

    def back_twist(rows, place, out):
        def piece(ks):
            parts = [twist_back(rows, cos_ref, sin_ref, place(k), k) for k in ks]
            store_rows(out, ks[0] * 8, [parts[0][0], parts[1][0]])
            if len(ks) == 3:
                store_rows(out, A * 8, [parts[2][0], parts[1][1]])
            else:
                store_rows(out, (A + ks[0]) * 8, [parts[0][1], parts[1][1]])

        return [lambda ks=ks: piece(ks) for ks in PAIRS]

    def results(g):
        def piece(half):
            cols = slice(half * 256, half * 256 + 256)
            state = mm(inv_ref[...], u_ref[g % 2, 0, :, cols]).reshape(A, 8, 256)
            back = mm(inv_ref[...], u_ref[g % 2, 1, :, cols]).reshape(A, 8, 256)
            both = jnp.concatenate([state, back], axis=1).astype(BF)
            for i in range(2):
                n = 2 * half + i
                out_ref[:, g, n * 16 : n * 16 + 16, :] = both[:, :, i * L : (i + 1) * L]

        return [lambda h=h: piece(h) for h in range(2)]

    def forward_rows(g):
        return row_sums(z_ref.at[g % 2], fr_ref, spec_ref.at[g % 2])

    def back_rows(g):
        return row_sums(y_ref.at[g % 2], ir_ref, v_ref.at[g % 2])

    def back_twists(g):
        pieces = []
        for f in range(2):
            pieces += back_twist(
                v_ref.at[g % 2], lambda k, f=f: k * 16 + f * 8, u_ref.at[g % 2, f]
            )
        return pieces

    def filter_sums():
        def piece(half):
            data = jnp.concatenate(
                [
                    up(in_ref[:, 2 * half + i, 64:72, :]).reshape(A * 8, L).astype(BF)
                    for i in range(2)
                ],
                axis=1,
            )
            filt_sums[:, half * 256 : half * 256 + 256] = mm(fwd_ref[...], data)

        return [lambda h=h: piece(h) for h in range(2)]

    def filter_twist():
        def piece(ks):
            found = [twist_forward([filt_sums], cos_ref, sin_ref, k)[0] for k in ks]
            store_rows(filt_z, ks[0] * 8, found)

        return [lambda ks=ks: piece(ks) for ks in [(k, k + 1) for k in range(0, A, 2)] + [(A,)]]

    def taps_rows():
        def piece(k):
            filt_z[k * 8 : k * 8 + 16, :] = taps_ref[k * 8 : k * 8 + 16, :].astype(BF)

        def last():
            filt_z[A * 8 :, :] = taps_ref[A * 8 :, :].astype(BF)

        return [lambda k=k: piece(k) for k in range(0, A, 2)] + [last]

    interleave(filter_sums() + block_sums(0), [])
    interleave(block_sums(1)[:2], filter_twist())
    interleave(row_sums(filt_z, fr_ref, filt_ref) + block_sums(1)[2:], forward_twist(0))
    for g in range(X):
        interleave(forward_rows(g), back_twists(g - 1) if g > 0 else [])
        interleave(results(g - 1) if g > 0 else [], products(g))
        interleave(back_rows(g), forward_twist(g + 1) if g + 1 < X else taps_rows())
        if g + 2 < X:
            interleave(block_sums(g + 2), [])
    interleave(row_sums(filt_z, ir_ref, filt_ref), back_twists(X - 1))
    interleave(results(X - 1), back_twist(filt_ref, lambda k: k * 8, u_ref.at[0, 0]))

    result = mm(inv_ref[...], u_ref[0, 0]) * (1.0 / 256.0)
    place = lax.broadcasted_iota(jnp.int32, (A * 8, L), 0) % 8 // 2
    for g in range(4):
        total = result[:, :L] if g == 0 else pltpu.roll(result[:, :L], (-2 * g) % (A * 8), 0)
        for n in range(1, 4):
            part = result[:, n * L : (n + 1) * L]
            moved = part if n == g else pltpu.roll(part, (2 * (n - g)) % (A * 8), 0)
            total = jnp.where(place == n, moved, total)
        out_ref[:, g, 64:72, :] = total.reshape(A, 8, L).astype(BF)


def transform(fields, t):
    return pl.pallas_call(
        transform_kernel,
        out_shape=jax.ShapeDtypeStruct((A, X, ROWS, L), BF),
        in_specs=[whole()] * 7,
        out_specs=whole(),
        scratch_shapes=[
            pltpu.VMEM((2, 2, 2 * KH * 8, SEG), F32),
            pltpu.VMEM((2, KH * 16, 2 * SEG), BF),
            pltpu.VMEM((2, KH * 16, 2 * SEG), F32),
            pltpu.VMEM((2, KH * 16, 2 * SEG), BF),
            pltpu.VMEM((2, KH * 16, 2 * SEG), F32),
            pltpu.VMEM((2, 2, 2 * A * 8, SEG), BF),
            pltpu.VMEM((2 * KH * 8, SEG), F32),
            pltpu.VMEM((KH * 8, 2 * SEG), BF),
            pltpu.VMEM((KH * 8, 2 * SEG), F32),
            pltpu.VMEM((KH * 8, 2 * SEG), F32),
        ],
        compiler_params=pltpu.CompilerParams(vmem_limit_bytes=36 * MIB),
        name="transform",
    )(
        fields, t["forward"], t["backward"], t["fwd_rows"], t["inv_rows"],
        t["cos_twist"], t["sin_twist"],
    )


def finish_kernel(
    in_ref, q_ref, k_ref, v_ref, o_ref, skip_ref, order_ref,
    dq_hbm, dk_hbm, dv_hbm, df_hbm,
    dq_ref, dk_ref, dv_ref, df_ref, field_sems, taps_sem,
):
    def in_place(rows):
        return lax.dot_general(
            rows.astype(BF), order_ref[...], (((0,), (0,)), ((), ())), preferred_element_type=F32
        )

    copies = []
    for n in range(4):
        here = slice(n * L, (n + 1) * L)
        for half in range(2):
            part = up(in_ref[half * 64 : half * 64 + 64, n * 16 : n * 16 + 16, :])
            rows = jnp.concatenate(
                [part[:, :8].reshape(512, L), part[:, 8:].reshape(512, L)], axis=1
            )
            conv = in_place(rows)
            for g in range(4):
                cols = slice(g * 256 + half * 128, g * 256 + half * 128 + 128)
                state = conv[:L, g * L : (g + 1) * L]
                back = conv[L:, g * L : (g + 1) * L]
                q, k, v, o = (up(ref[here, cols]) for ref in (q_ref, k_ref, v_ref, o_ref))
                skip = skip_ref[:, cols]
                mixed = state + skip * up((k * v).astype(BF))
                total = back + skip * up((q * o).astype(BF))
                dq_ref[here, cols] = (o * mixed).astype(BF)
                dk_ref[here, cols] = (total * v).astype(BF)
                dv_ref[here, cols] = (total * k).astype(BF)
        if n == 1:
            for half in range(2):
                rows = up(in_ref[half * 64 : half * 64 + 64, 64:72, :]).reshape(512, L)
                taps = in_place(rows)
                for m in range(4):
                    df_ref[m * L : (m + 1) * L, half * 128 : half * 128 + 128] = taps[
                        :, m * L : (m + 1) * L
                    ]
            copies.append(pltpu.make_async_copy(df_ref, df_hbm, taps_sem))
            copies[-1].start()
        pairs = ((dq_ref, dq_hbm), (dk_ref, dk_hbm), (dv_ref, dv_hbm))
        for i, (source, target) in enumerate(pairs):
            rows = pl.ds(n * L, L)
            copies.append(
                pltpu.make_async_copy(source.at[rows], target.at[rows], field_sems.at[n, i])
            )
            copies[-1].start()
    for copy in copies:
        copy.wait()


def finish(fields, q_in, k_in, v_in, out_grad, skip, order):
    return pl.pallas_call(
        finish_kernel,
        out_shape=(
            jax.ShapeDtypeStruct((SEG, 1024), BF),
            jax.ShapeDtypeStruct((SEG, 1024), BF),
            jax.ShapeDtypeStruct((SEG, 1024), BF),
            jax.ShapeDtypeStruct((SEG, 256), F32),
        ),
        in_specs=[whole()] * 7,
        out_specs=(pl.BlockSpec(memory_space=pl.ANY),) * 4,
        scratch_shapes=[
            pltpu.VMEM((SEG, 1024), BF),
            pltpu.VMEM((SEG, 1024), BF),
            pltpu.VMEM((SEG, 1024), BF),
            pltpu.VMEM((SEG, 256), F32),
            pltpu.SemaphoreType.DMA((4, 3)),
            pltpu.SemaphoreType.DMA,
        ],
        compiler_params=pltpu.CompilerParams(vmem_limit_bytes=24 * MIB),
        name="finish",
    )(fields, q_in, k_in, v_in, out_grad, skip, order)


def body(q_in, k_in, v_in, out_grad, filters, skip):
    t = {name: jnp.asarray(value) for name, value in constants().items()}
    sent = pack(q_in, k_in, v_in, out_grad, filters)
    columns = lax.all_to_all(sent, ("ctx", "ch"), split_axis=0, concat_axis=0, tiled=True)
    results = transform(columns.reshape(A, X, ROWS, L), t)
    blocks = lax.all_to_all(
        results.reshape(DEV, ROWS, L), ("ctx", "ch"), split_axis=0, concat_axis=0, tiled=True
    )
    return finish(blocks, q_in, k_in, v_in, out_grad, skip.reshape(1, 1024), t["order"])


def solution(mesh):
    return jax.shard_map(
        body,
        mesh=mesh,
        in_specs=(
            P("ctx", "ch"),
            P("ctx", "ch"),
            P("ctx", "ch"),
            P("ctx", "ch"),
            P("ctx", None),
            P("ch"),
        ),
        out_specs=(P("ctx", "ch"), P("ctx", "ch"), P("ctx", "ch"), P("ctx", "ch")),
        check_vma=False,
    )
```

```python
import functools
import math

import jax
import jax.numpy as jnp
import ml_dtypes
import numpy as np
from jax import lax
from jax.experimental import pallas as pl
from jax.experimental.pallas import tpu as pltpu
from jax.sharding import PartitionSpec as P

BF = jnp.bfloat16
F32 = jnp.float32

A = 32
X = 4
DEV = A * X
L = 128
SEG = 4 * L
KH = A + 1
PERIOD = 2 * A * SEG
ROWS = 72
MIB = 1024 * 1024


def low(table):
    return np.asarray(table, np.float32).astype(ml_dtypes.bfloat16)


def spread(table, count):
    return np.kron(table, np.eye(count))


@functools.cache
def constants():
    k = np.arange(KH)[:, None]
    a = np.arange(A)[None, :]
    angle = 2 * np.pi * (k * a % (2 * A)) / (2 * A)
    cos_block = low(np.cos(angle)).astype(np.float64)
    sin_block = low(np.sin(angle)).astype(np.float64)
    cos_block[np.abs(cos_block) < 1e-6] = 0.0
    sin_block[np.abs(sin_block) < 1e-6] = 0.0
    forward = np.stack([cos_block, -sin_block], 1).reshape(2 * KH, A)
    weight = np.where((k == 0) | (k == A), 1.0, 2.0) / PERIOD
    backward = np.concatenate([weight * cos_block, -(weight * sin_block)[1:A]], 0).T
    l = np.arange(L)[:, None]
    fwd_rows, inv_rows = [], []
    for r in range(4):
        q = r + 4 * np.arange(L)[None, :]
        angle = 2 * np.pi * (l * q % SEG) / SEG
        c, s = np.cos(angle), np.sin(angle)
        fwd_rows.append(np.block([[c, -s], [s, c]]))
        inv_rows.append(np.block([[c.T, s.T], [-s.T, c.T]]))
    j = np.arange(SEG)[None, :]
    twist = 2 * np.pi * (k * j % PERIOD) / PERIOD
    row = np.arange(512)
    column = (row // 2) % 4 * 128 + row // 8 * 2 + row % 2
    order = np.zeros((512, 512))
    order[row, column] = 1.0
    return {
        "forward": low(spread(forward, 8)),
        "backward": low(spread(backward, 8)),
        "fwd_rows": low(np.stack(fwd_rows)),
        "inv_rows": low(np.stack(inv_rows)),
        "cos_twist": np.cos(twist).astype(np.float32),
        "sin_twist": np.sin(twist).astype(np.float32),
        "order": low(order),
    }


def mm(left, right):
    return jnp.dot(left, right, preferred_element_type=F32)


def up(value):
    return value.astype(F32)


def whole():
    return pl.BlockSpec(memory_space=pltpu.VMEM)


def pack_kernel(
    q_hbm, k_hbm, v_hbm, o_hbm, f_hbm, out_hbm,
    fields_ref, taps_ref, order_ref, pair_ref, tail_ref, field_sems, taps_sem, out_sems,
):
    sources = (k_hbm, v_hbm, q_hbm, o_hbm)

    def field_copy(i, n):
        rows = pl.ds(n * L, L)
        return pltpu.make_async_copy(
            sources[i].at[rows], fields_ref.at[i, rows], field_sems.at[n, i]
        )

    rows = pl.ds(pl.multiple_of(lax.axis_index("ch") * L, L), L)
    taps_copy = pltpu.make_async_copy(f_hbm.at[rows], taps_ref, taps_sem)
    for n in range(4):
        for i in range(4):
            field_copy(i, n).start()
    taps_copy.start()
    row = lax.broadcasted_iota(jnp.int32, (512, 512), 0)
    column = lax.broadcasted_iota(jnp.int32, (512, 512), 1)
    source = row // 2 % 4 * 128 + row // 8 * 2 + row % 2
    order_ref[...] = jnp.where(column == source, 1.0, 0.0).astype(BF)

    def by_owner(field, half):
        columns = jnp.concatenate(
            [field[:, g * 256 + half * 128 : g * 256 + half * 128 + 128] for g in range(4)], axis=1
        )
        return lax.dot_general(
            order_ref[...], columns, (((1,), (1,)), ((), ())), preferred_element_type=F32
        )

    copies = []
    for n in range(4):
        for i in range(4):
            field_copy(i, n).wait()
        k, v, q, o = (up(fields_ref[i, n * L : (n + 1) * L, :]) for i in range(4))
        both = jnp.concatenate([(k * v).astype(BF), (q * o).astype(BF)], axis=0)
        for half in range(2):
            moved = by_owner(both, half)
            pair = jnp.concatenate(
                [moved[:, :L].reshape(64, 8, L), moved[:, L:].reshape(64, 8, L)], axis=1
            )
            pair_ref[n, half * 64 : half * 64 + 64, :, :] = pair.astype(BF)
        copies.append(
            pltpu.make_async_copy(
                pair_ref.at[n], out_hbm.at[:, pl.ds(n * 16, 16), :], out_sems.at[n]
            )
        )
        copies[-1].start()
    taps_copy.wait()
    taps = taps_ref[...].astype(BF)
    for half in range(2):
        moved = by_owner(taps, half).reshape(64, 8, L)
        tail_ref[half * 64 : half * 64 + 64, :, :] = moved.astype(BF)
    copies.append(
        pltpu.make_async_copy(tail_ref, out_hbm.at[:, pl.ds(64, 8), :], out_sems.at[4])
    )
    copies[-1].start()
    for copy in copies:
        copy.wait()


def pack(q_in, k_in, v_in, out_grad, filters):
    return pl.pallas_call(
        pack_kernel,
        out_shape=jax.ShapeDtypeStruct((DEV, ROWS, L), BF),
        in_specs=[pl.BlockSpec(memory_space=pl.ANY)] * 5,
        out_specs=pl.BlockSpec(memory_space=pl.ANY),
        scratch_shapes=[
            pltpu.VMEM((4, SEG, 1024), BF),
            pltpu.VMEM((L, 1024), F32),
            pltpu.VMEM((512, 512), BF),
            pltpu.VMEM((4, DEV, 16, L), BF),
            pltpu.VMEM((DEV, 8, L), BF),
            pltpu.SemaphoreType.DMA((4, 4)),
            pltpu.SemaphoreType.DMA,
            pltpu.SemaphoreType.DMA((5,)),
        ],
        compiler_params=pltpu.CompilerParams(vmem_limit_bytes=60 * MIB),
        name="pack",
    )(q_in, k_in, v_in, out_grad, filters)


def quarters(value):
    return [value[:, i * L : (i + 1) * L] for i in range(4)]


def butterfly(re, im, sign):
    ar, br, cr, dr = re[0] + re[2], re[0] - re[2], re[1] + re[3], re[1] - re[3]
    ai, bi, ci, di = im[0] + im[2], im[0] - im[2], im[1] + im[3], im[1] - im[3]
    plus = (br - di, bi + dr)
    minus = (br + di, bi - dr)
    first, third = (plus, minus) if sign > 0 else (minus, plus)
    return [(ar + cr, ai + ci), first, (ar - cr, ai - ci), third]


def twist_forward(fields, cos_ref, sin_ref, k):
    c = cos_ref[k : k + 1, :]
    s = sin_ref[k : k + 1, :]
    found = []
    for sums_ref in fields:
        both = up(sums_ref[k * 16 : k * 16 + 16, :])
        re, im = both[:8], both[8:]
        parts = butterfly(quarters(re * c + im * s), quarters(im * c - re * s), -1)
        found.append(jnp.concatenate([part for pair in parts for part in pair], axis=1))
    return found


def store_rows(ref, row, pieces):
    ref[row : row + 8 * len(pieces), :] = jnp.concatenate(pieces, axis=0).astype(BF)


def twist_back(rows_ref, cos_ref, sin_ref, rows, k):
    re = [up(rows_ref[rows, n * 256 : n * 256 + L]) for n in range(4)]
    im = [up(rows_ref[rows, n * 256 + L : n * 256 + 256]) for n in range(4)]
    real, imag = [], []
    for n, (ur, ui) in enumerate(butterfly(re, im, 1)):
        c = cos_ref[k : k + 1, n * L : (n + 1) * L]
        s = sin_ref[k : k + 1, n * L : (n + 1) * L]
        real.append(ur * c - ui * s)
        imag.append(ui * c + ur * s)
    return jnp.concatenate(real, axis=1), jnp.concatenate(imag, axis=1)


def interleave(first, second):
    n, m = len(first), len(second)
    if n == 0 or m == 0:
        order = list(first) + list(second)
    else:
        order = []
        done = 0
        for i, piece in enumerate(first):
            order.append(piece)
            upto = (i + 1) * m // n
            order.extend(second[done:upto])
            done = upto
    for piece in order:
        piece()


PAIRS = [(0, 1, A)] + [(k, k + 1) for k in range(2, A, 2)]


def transform_kernel(
    in_ref, fwd_ref, inv_ref, fr_ref, ir_ref, cos_ref, sin_ref, out_ref,
    sums_ref, z_ref, spec_ref, y_ref, v_ref, u_ref, filt_sums, filt_z, filt_ref, taps_ref,
):
    def load(g, n, field):
        rows = up(in_ref[:, g, n * 16 : n * 16 + 16, :])
        return rows[:, field * 8 : field * 8 + 8].reshape(A * 8, L).astype(BF)

    def block_sums(g):
        def piece(field, half):
            data = jnp.concatenate([load(g, 2 * half + i, field) for i in range(2)], axis=1)
            sums_ref[g % 2, field, :, half * 256 : half * 256 + 256] = mm(fwd_ref[...], data)

        return [lambda f=f, h=h: piece(f, h) for f in range(2) for h in range(2)]

    def forward_twist(g):
        def piece(k):
            fields = [sums_ref.at[g % 2, 0], sums_ref.at[g % 2, 1]]
            store_rows(z_ref.at[g % 2], k * 16, twist_forward(fields, cos_ref, sin_ref, k))

        return [lambda k=k: piece(k) for k in range(KH)]

    def row_sums(data, table, out):
        def piece(n):
            cols = slice(n * 256, (n + 1) * 256)
            out[:, cols] = mm(data[:, cols], table[n]).astype(out.dtype)

        return [lambda n=n: piece(n) for n in range(4)]

    def products(g):
        def piece(k):
            spec, y = spec_ref.at[g % 2], y_ref.at[g % 2]
            r8 = slice(k * 8, k * 8 + 8)
            rg = slice(k * 16, k * 16 + 8)
            rr = slice(k * 16 + 8, k * 16 + 16)
            for n in range(4):
                re = slice(n * 256, n * 256 + L)
                im = slice(n * 256 + L, n * 256 + 256)
                fr, fi = filt_ref[r8, re], filt_ref[r8, im]
                gr, gi = spec[rg, re], spec[rg, im]
                hr, hi = spec[rr, re], spec[rr, im]
                wr = hr * gr + hi * gi
                wi = hi * gr - hr * gi
                if g > 0:
                    wr = wr + taps_ref[r8, re]
                    wi = wi + taps_ref[r8, im]
                taps_ref[r8, re] = wr
                taps_ref[r8, im] = wi
                rows = slice(k * 16, k * 16 + 16)
                y[rows, re] = jnp.concatenate(
                    [gr * fr - gi * fi, hr * fr + hi * fi], axis=0
                ).astype(BF)
                y[rows, im] = jnp.concatenate(
                    [gr * fi + gi * fr, hi * fr - hr * fi], axis=0
                ).astype(BF)

        return [lambda k=k: piece(k) for k in range(KH)]

    def back_twist(rows, height, outs):
        def piece(ks):
            parts = [
                twist_back(rows, cos_ref, sin_ref, slice(k * height, (k + 1) * height), k)
                for k in ks
            ]
            for i, out in enumerate(outs):
                own = [(re[i * 8 : i * 8 + 8], im[i * 8 : i * 8 + 8]) for re, im in parts]
                store_rows(out, ks[0] * 8, [own[0][0], own[1][0]])
                if len(ks) == 3:
                    store_rows(out, A * 8, [own[2][0], own[1][1]])
                else:
                    store_rows(out, (A + ks[0]) * 8, [own[0][1], own[1][1]])

        return [lambda ks=ks: piece(ks) for ks in PAIRS]

    def results(g):
        def piece(half):
            cols = slice(half * 256, half * 256 + 256)
            state = mm(inv_ref[...], u_ref[g % 2, 0, :, cols]).reshape(A, 8, 256)
            back = mm(inv_ref[...], u_ref[g % 2, 1, :, cols]).reshape(A, 8, 256)
            both = jnp.concatenate([state, back], axis=1).astype(BF)
            for i in range(2):
                n = 2 * half + i
                out_ref[:, g, n * 16 : n * 16 + 16, :] = both[:, :, i * L : (i + 1) * L]

        return [lambda h=h: piece(h) for h in range(2)]

    def forward_rows(g):
        return row_sums(z_ref.at[g % 2], fr_ref, spec_ref.at[g % 2])

    def back_rows(g):
        return row_sums(y_ref.at[g % 2], ir_ref, v_ref.at[g % 2])

    def back_twists(g):
        return back_twist(v_ref.at[g % 2], 16, [u_ref.at[g % 2, f] for f in range(2)])

    def filter_sums():
        def piece(half):
            data = jnp.concatenate(
                [
                    up(in_ref[:, 2 * half + i, 64:72, :]).reshape(A * 8, L).astype(BF)
                    for i in range(2)
                ],
                axis=1,
            )
            filt_sums[:, half * 256 : half * 256 + 256] = mm(fwd_ref[...], data)

        return [lambda h=h: piece(h) for h in range(2)]

    def filter_twist():
        def piece(ks):
            found = [twist_forward([filt_sums], cos_ref, sin_ref, k)[0] for k in ks]
            store_rows(filt_z, ks[0] * 8, found)

        return [lambda ks=ks: piece(ks) for ks in [(k, k + 1) for k in range(0, A, 2)] + [(A,)]]

    def taps_rows():
        def piece(k):
            filt_z[k * 8 : k * 8 + 16, :] = taps_ref[k * 8 : k * 8 + 16, :].astype(BF)

        def last():
            filt_z[A * 8 :, :] = taps_ref[A * 8 :, :].astype(BF)

        return [lambda k=k: piece(k) for k in range(0, A, 2)] + [last]

    interleave(filter_sums() + block_sums(0), [])
    interleave(block_sums(1)[:2], filter_twist())
    interleave(row_sums(filt_z, fr_ref, filt_ref) + block_sums(1)[2:], forward_twist(0))
    for g in range(X):
        interleave(forward_rows(g), back_twists(g - 1) if g > 0 else [])
        interleave(results(g - 1) if g > 0 else [], products(g))
        interleave(back_rows(g), forward_twist(g + 1) if g + 1 < X else taps_rows())
        if g + 2 < X:
            interleave(block_sums(g + 2), [])
    interleave(row_sums(filt_z, ir_ref, filt_ref), back_twists(X - 1))
    interleave(results(X - 1), back_twist(filt_ref, 8, [u_ref.at[0, 0]]))

    result = mm(inv_ref[...], u_ref[0, 0]) * (1.0 / 256.0)
    place = lax.broadcasted_iota(jnp.int32, (A * 8, L), 0) % 8 // 2
    for g in range(4):
        total = result[:, :L] if g == 0 else pltpu.roll(result[:, :L], (-2 * g) % (A * 8), 0)
        for n in range(1, 4):
            part = result[:, n * L : (n + 1) * L]
            moved = part if n == g else pltpu.roll(part, (2 * (n - g)) % (A * 8), 0)
            total = jnp.where(place == n, moved, total)
        out_ref[:, g, 64:72, :] = total.reshape(A, 8, L).astype(BF)


def transform(fields, t):
    return pl.pallas_call(
        transform_kernel,
        out_shape=jax.ShapeDtypeStruct((A, X, ROWS, L), BF),
        in_specs=[whole()] * 7,
        out_specs=whole(),
        scratch_shapes=[
            pltpu.VMEM((2, 2, 2 * KH * 8, SEG), F32),
            pltpu.VMEM((2, KH * 16, 2 * SEG), BF),
            pltpu.VMEM((2, KH * 16, 2 * SEG), F32),
            pltpu.VMEM((2, KH * 16, 2 * SEG), BF),
            pltpu.VMEM((2, KH * 16, 2 * SEG), F32),
            pltpu.VMEM((2, 2, 2 * A * 8, SEG), BF),
            pltpu.VMEM((2 * KH * 8, SEG), F32),
            pltpu.VMEM((KH * 8, 2 * SEG), BF),
            pltpu.VMEM((KH * 8, 2 * SEG), F32),
            pltpu.VMEM((KH * 8, 2 * SEG), F32),
        ],
        compiler_params=pltpu.CompilerParams(vmem_limit_bytes=36 * MIB),
        name="transform",
    )(
        fields, t["forward"], t["backward"], t["fwd_rows"], t["inv_rows"],
        t["cos_twist"], t["sin_twist"],
    )


def finish_kernel(
    in_ref, q_ref, k_ref, v_ref, o_ref, skip_ref, order_ref,
    dq_hbm, dk_hbm, dv_hbm, df_hbm,
    dq_ref, dk_ref, dv_ref, df_ref, field_sems, taps_sem,
):
    def in_place(rows):
        return lax.dot_general(
            rows.astype(BF), order_ref[...], (((0,), (0,)), ((), ())), preferred_element_type=F32
        )

    copies = []
    for n in range(4):
        here = slice(n * L, (n + 1) * L)
        for half in range(2):
            part = up(in_ref[half * 64 : half * 64 + 64, n * 16 : n * 16 + 16, :])
            rows = jnp.concatenate(
                [part[:, :8].reshape(512, L), part[:, 8:].reshape(512, L)], axis=1
            )
            conv = in_place(rows)
            for g in range(4):
                cols = slice(g * 256 + half * 128, g * 256 + half * 128 + 128)
                state = conv[:L, g * L : (g + 1) * L]
                back = conv[L:, g * L : (g + 1) * L]
                q, k, v, o = (up(ref[here, cols]) for ref in (q_ref, k_ref, v_ref, o_ref))
                skip = skip_ref[:, cols]
                mixed = state + skip * up((k * v).astype(BF))
                total = back + skip * up((q * o).astype(BF))
                dq_ref[here, cols] = (o * mixed).astype(BF)
                dk_ref[here, cols] = (total * v).astype(BF)
                dv_ref[here, cols] = (total * k).astype(BF)
        if n == 1:
            for half in range(2):
                rows = up(in_ref[half * 64 : half * 64 + 64, 64:72, :]).reshape(512, L)
                taps = in_place(rows)
                for m in range(4):
                    df_ref[m * L : (m + 1) * L, half * 128 : half * 128 + 128] = taps[
                        :, m * L : (m + 1) * L
                    ]
            copies.append(pltpu.make_async_copy(df_ref, df_hbm, taps_sem))
            copies[-1].start()
        pairs = ((dq_ref, dq_hbm), (dk_ref, dk_hbm), (dv_ref, dv_hbm))
        for i, (source, target) in enumerate(pairs):
            rows = pl.ds(n * L, L)
            copies.append(
                pltpu.make_async_copy(source.at[rows], target.at[rows], field_sems.at[n, i])
            )
            copies[-1].start()
    for copy in copies:
        copy.wait()


def finish(fields, q_in, k_in, v_in, out_grad, skip, order):
    return pl.pallas_call(
        finish_kernel,
        out_shape=(
            jax.ShapeDtypeStruct((SEG, 1024), BF),
            jax.ShapeDtypeStruct((SEG, 1024), BF),
            jax.ShapeDtypeStruct((SEG, 1024), BF),
            jax.ShapeDtypeStruct((SEG, 256), F32),
        ),
        in_specs=[whole()] * 7,
        out_specs=(pl.BlockSpec(memory_space=pl.ANY),) * 4,
        scratch_shapes=[
            pltpu.VMEM((SEG, 1024), BF),
            pltpu.VMEM((SEG, 1024), BF),
            pltpu.VMEM((SEG, 1024), BF),
            pltpu.VMEM((SEG, 256), F32),
            pltpu.SemaphoreType.DMA((4, 3)),
            pltpu.SemaphoreType.DMA,
        ],
        compiler_params=pltpu.CompilerParams(vmem_limit_bytes=24 * MIB),
        name="finish",
    )(fields, q_in, k_in, v_in, out_grad, skip, order)


def body(q_in, k_in, v_in, out_grad, filters, skip):
    t = {name: jnp.asarray(value) for name, value in constants().items()}
    sent = pack(q_in, k_in, v_in, out_grad, filters)
    columns = lax.all_to_all(sent, ("ctx", "ch"), split_axis=0, concat_axis=0, tiled=True)
    results = transform(columns.reshape(A, X, ROWS, L), t)
    blocks = lax.all_to_all(
        results.reshape(DEV, ROWS, L), ("ctx", "ch"), split_axis=0, concat_axis=0, tiled=True
    )
    return finish(blocks, q_in, k_in, v_in, out_grad, skip.reshape(1, 1024), t["order"])


def solution(mesh):
    return jax.shard_map(
        body,
        mesh=mesh,
        in_specs=(
            P("ctx", "ch"),
            P("ctx", "ch"),
            P("ctx", "ch"),
            P("ctx", "ch"),
            P("ctx", None),
            P("ch"),
        ),
        out_specs=(P("ctx", "ch"), P("ctx", "ch"), P("ctx", "ch"), P("ctx", "ch")),
        check_vma=False,
    )
```

```python
import functools
import math

import jax
import jax.numpy as jnp
import ml_dtypes
import numpy as np
from jax import lax
from jax.experimental import pallas as pl
from jax.experimental.pallas import tpu as pltpu
from jax.sharding import PartitionSpec as P

BF = jnp.bfloat16
F32 = jnp.float32

A = 32
X = 4
DEV = A * X
L = 128
SEG = 4 * L
KH = A + 1
PERIOD = 2 * A * SEG
ROWS = 72
MIB = 1024 * 1024


def low(table):
    return np.asarray(table, np.float32).astype(ml_dtypes.bfloat16)


def spread(table, count):
    return np.kron(table, np.eye(count))


@functools.cache
def constants():
    k = np.arange(KH)[:, None]
    a = np.arange(A)[None, :]
    angle = 2 * np.pi * (k * a % (2 * A)) / (2 * A)
    cos_block = low(np.cos(angle)).astype(np.float64)
    sin_block = low(np.sin(angle)).astype(np.float64)
    cos_block[np.abs(cos_block) < 1e-6] = 0.0
    sin_block[np.abs(sin_block) < 1e-6] = 0.0
    forward = np.stack([cos_block, -sin_block], 1).reshape(2 * KH, A)
    weight = np.where((k == 0) | (k == A), 1.0, 2.0) / PERIOD
    backward = np.concatenate([weight * cos_block, -(weight * sin_block)[1:A]], 0).T
    l = np.arange(L)[:, None]
    fwd_rows, inv_rows = [], []
    for r in range(4):
        q = r + 4 * np.arange(L)[None, :]
        angle = 2 * np.pi * (l * q % SEG) / SEG
        c, s = np.cos(angle), np.sin(angle)
        fwd_rows.append(np.block([[c, -s], [s, c]]))
        inv_rows.append(np.block([[c.T, s.T], [-s.T, c.T]]))
    j = np.arange(SEG)[None, :]
    twist = 2 * np.pi * (k * j % PERIOD) / PERIOD
    row = np.arange(512)
    column = (row // 2) % 4 * 128 + row // 8 * 2 + row % 2
    order = np.zeros((512, 512))
    order[row, column] = 1.0
    return {
        "forward": low(spread(forward, 8)),
        "backward": low(spread(backward, 8)),
        "fwd_rows": low(np.stack(fwd_rows)),
        "inv_rows": low(np.stack(inv_rows)),
        "cos_twist": np.cos(twist).astype(np.float32),
        "sin_twist": np.sin(twist).astype(np.float32),
        "order": low(order),
    }


def mm(left, right):
    return jnp.dot(left, right, preferred_element_type=F32)


def up(value):
    return value.astype(F32)


def whole():
    return pl.BlockSpec(memory_space=pltpu.VMEM)


def pack_kernel(
    q_hbm, k_hbm, v_hbm, o_hbm, f_hbm, out_hbm,
    fields_ref, taps_ref, order_ref, pair_ref, tail_ref, field_sems, taps_sem, out_sems,
):
    sources = (k_hbm, v_hbm, q_hbm, o_hbm)

    def field_copy(i, n):
        rows = pl.ds(n * L, 2 * L if n == 2 else L)
        return pltpu.make_async_copy(
            sources[i].at[rows], fields_ref.at[i, rows], field_sems.at[n, i]
        )

    rows = pl.ds(pl.multiple_of(lax.axis_index("ch") * L, L), L)
    taps_copy = pltpu.make_async_copy(f_hbm.at[rows], taps_ref, taps_sem)
    for n in range(3):
        for i in range(4):
            field_copy(i, n).start()
    taps_copy.start()
    row = lax.broadcasted_iota(jnp.int32, (512, 512), 0)
    column = lax.broadcasted_iota(jnp.int32, (512, 512), 1)
    source = row // 2 % 4 * 128 + row // 8 * 2 + row % 2
    order_ref[...] = jnp.where(column == source, 1.0, 0.0).astype(BF)

    def by_owner(field, half):
        columns = jnp.concatenate(
            [field[:, g * 256 + half * 128 : g * 256 + half * 128 + 128] for g in range(4)], axis=1
        )
        return lax.dot_general(
            order_ref[...], columns, (((1,), (1,)), ((), ())), preferred_element_type=F32
        )

    copies = []
    for n in range(4):
        for i in range(4 if n < 3 else 0):
            field_copy(i, n).wait()
        k, v, q, o = (up(fields_ref[i, n * L : (n + 1) * L, :]) for i in range(4))
        both = jnp.concatenate([(k * v).astype(BF), (q * o).astype(BF)], axis=0)
        for half in range(2):
            moved = by_owner(both, half)
            pair = jnp.concatenate(
                [moved[:, :L].reshape(64, 8, L), moved[:, L:].reshape(64, 8, L)], axis=1
            )
            pair_ref[n, half * 64 : half * 64 + 64, :, :] = pair.astype(BF)
        copies.append(
            pltpu.make_async_copy(
                pair_ref.at[n], out_hbm.at[:, pl.ds(n * 16, 16), :], out_sems.at[n]
            )
        )
        copies[-1].start()
    taps_copy.wait()
    taps = taps_ref[...].astype(BF)
    for half in range(2):
        moved = by_owner(taps, half).reshape(64, 8, L)
        tail_ref[half * 64 : half * 64 + 64, :, :] = moved.astype(BF)
    copies.append(
        pltpu.make_async_copy(tail_ref, out_hbm.at[:, pl.ds(64, 8), :], out_sems.at[4])
    )
    copies[-1].start()
    for copy in copies:
        copy.wait()


def pack(q_in, k_in, v_in, out_grad, filters):
    return pl.pallas_call(
        pack_kernel,
        out_shape=jax.ShapeDtypeStruct((DEV, ROWS, L), BF),
        in_specs=[pl.BlockSpec(memory_space=pl.ANY)] * 5,
        out_specs=pl.BlockSpec(memory_space=pl.ANY),
        scratch_shapes=[
            pltpu.VMEM((4, SEG, 1024), BF),
            pltpu.VMEM((L, 1024), F32),
            pltpu.VMEM((512, 512), BF),
            pltpu.VMEM((4, DEV, 16, L), BF),
            pltpu.VMEM((DEV, 8, L), BF),
            pltpu.SemaphoreType.DMA((3, 4)),
            pltpu.SemaphoreType.DMA,
            pltpu.SemaphoreType.DMA((5,)),
        ],
        compiler_params=pltpu.CompilerParams(vmem_limit_bytes=60 * MIB),
        name="pack",
    )(q_in, k_in, v_in, out_grad, filters)


def quarters(value):
    return [value[:, i * L : (i + 1) * L] for i in range(4)]


def butterfly(re, im, sign):
    ar, br, cr, dr = re[0] + re[2], re[0] - re[2], re[1] + re[3], re[1] - re[3]
    ai, bi, ci, di = im[0] + im[2], im[0] - im[2], im[1] + im[3], im[1] - im[3]
    plus = (br - di, bi + dr)
    minus = (br + di, bi - dr)
    first, third = (plus, minus) if sign > 0 else (minus, plus)
    return [(ar + cr, ai + ci), first, (ar - cr, ai - ci), third]


def twist_forward(fields, cos_ref, sin_ref, k):
    c = cos_ref[k : k + 1, :]
    s = sin_ref[k : k + 1, :]
    found = []
    for sums_ref in fields:
        both = up(sums_ref[k * 16 : k * 16 + 16, :])
        re, im = both[:8], both[8:]
        parts = butterfly(quarters(re * c + im * s), quarters(im * c - re * s), -1)
        found.append(jnp.concatenate([part for pair in parts for part in pair], axis=1))
    return found


def store_rows(ref, row, pieces):
    ref[row : row + 8 * len(pieces), :] = jnp.concatenate(pieces, axis=0).astype(BF)


def twist_back(rows_ref, cos_ref, sin_ref, rows, k):
    re = [up(rows_ref[rows, n * 256 : n * 256 + L]) for n in range(4)]
    im = [up(rows_ref[rows, n * 256 + L : n * 256 + 256]) for n in range(4)]
    real, imag = [], []
    for n, (ur, ui) in enumerate(butterfly(re, im, 1)):
        c = cos_ref[k : k + 1, n * L : (n + 1) * L]
        s = sin_ref[k : k + 1, n * L : (n + 1) * L]
        real.append(ur * c - ui * s)
        imag.append(ui * c + ur * s)
    return jnp.concatenate(real, axis=1), jnp.concatenate(imag, axis=1)


def interleave(first, second):
    n, m = len(first), len(second)
    if n == 0 or m == 0:
        order = list(first) + list(second)
    else:
        order = []
        done = 0
        for i, piece in enumerate(first):
            order.append(piece)
            upto = (i + 1) * m // n
            order.extend(second[done:upto])
            done = upto
    for piece in order:
        piece()


PAIRS = [(0, 1, A)] + [(k, k + 1) for k in range(2, A, 2)]


def transform_kernel(
    in_ref, fwd_ref, inv_ref, fr_ref, ir_ref, cos_ref, sin_ref, out_ref,
    sums_ref, z_ref, spec_ref, y_ref, v_ref, u_ref, filt_sums, filt_z, filt_ref, taps_ref,
):
    def load(g, n, field):
        rows = up(in_ref[:, g, n * 16 : n * 16 + 16, :])
        return rows[:, field * 8 : field * 8 + 8].reshape(A * 8, L).astype(BF)

    def block_sums(g):
        def piece(field, half):
            data = jnp.concatenate([load(g, 2 * half + i, field) for i in range(2)], axis=1)
            sums_ref[g % 2, field, :, half * 256 : half * 256 + 256] = mm(fwd_ref[...], data)

        return [lambda f=f, h=h: piece(f, h) for f in range(2) for h in range(2)]

    def forward_twist(g):
        def piece(k):
            fields = [sums_ref.at[g % 2, 0], sums_ref.at[g % 2, 1]]
            store_rows(z_ref.at[g % 2], k * 16, twist_forward(fields, cos_ref, sin_ref, k))

        return [lambda k=k: piece(k) for k in range(KH)]

    def row_sums(data, table, out):
        def piece(n):
            cols = slice(n * 256, (n + 1) * 256)
            out[:, cols] = mm(data[:, cols], table[n]).astype(out.dtype)

        return [lambda n=n: piece(n) for n in range(4)]

    def products(g):
        def piece(k):
            spec, y = spec_ref.at[g % 2], y_ref.at[g % 2]
            r8 = slice(k * 8, k * 8 + 8)
            rg = slice(k * 16, k * 16 + 8)
            rr = slice(k * 16 + 8, k * 16 + 16)
            for n in range(4):
                re = slice(n * 256, n * 256 + L)
                im = slice(n * 256 + L, n * 256 + 256)
                fr, fi = filt_ref[r8, re], filt_ref[r8, im]
                gr, gi = spec[rg, re], spec[rg, im]
                hr, hi = spec[rr, re], spec[rr, im]
                wr = hr * gr + hi * gi
                wi = hi * gr - hr * gi
                if g > 0:
                    wr = wr + taps_ref[r8, re]
                    wi = wi + taps_ref[r8, im]
                taps_ref[r8, re] = wr
                taps_ref[r8, im] = wi
                rows = slice(k * 16, k * 16 + 16)
                y[rows, re] = jnp.concatenate(
                    [gr * fr - gi * fi, hr * fr + hi * fi], axis=0
                ).astype(BF)
                y[rows, im] = jnp.concatenate(
                    [gr * fi + gi * fr, hi * fr - hr * fi], axis=0
                ).astype(BF)

        return [lambda k=k: piece(k) for k in range(KH)]

    def back_twist(rows, height, outs):
        def piece(ks):
            parts = [
                twist_back(rows, cos_ref, sin_ref, slice(k * height, (k + 1) * height), k)
                for k in ks
            ]
            for i, out in enumerate(outs):
                own = [(re[i * 8 : i * 8 + 8], im[i * 8 : i * 8 + 8]) for re, im in parts]
                store_rows(out, ks[0] * 8, [own[0][0], own[1][0]])
                if len(ks) == 3:
                    store_rows(out, A * 8, [own[2][0], own[1][1]])
                else:
                    store_rows(out, (A + ks[0]) * 8, [own[0][1], own[1][1]])

        return [lambda ks=ks: piece(ks) for ks in PAIRS]

    def results(g):
        def piece(half):
            cols = slice(half * 256, half * 256 + 256)
            state = mm(inv_ref[...], u_ref[g % 2, 0, :, cols]).reshape(A, 8, 256)
            back = mm(inv_ref[...], u_ref[g % 2, 1, :, cols]).reshape(A, 8, 256)
            both = jnp.concatenate([state, back], axis=1).astype(BF)
            for i in range(2):
                n = 2 * half + i
                out_ref[:, g, n * 16 : n * 16 + 16, :] = both[:, :, i * L : (i + 1) * L]

        return [lambda h=h: piece(h) for h in range(2)]

    def forward_rows(g):
        return row_sums(z_ref.at[g % 2], fr_ref, spec_ref.at[g % 2])

    def back_rows(g):
        return row_sums(y_ref.at[g % 2], ir_ref, v_ref.at[g % 2])

    def back_twists(g):
        return back_twist(v_ref.at[g % 2], 16, [u_ref.at[g % 2, f] for f in range(2)])

    def filter_sums():
        def piece(half):
            data = jnp.concatenate(
                [
                    up(in_ref[:, 2 * half + i, 64:72, :]).reshape(A * 8, L).astype(BF)
                    for i in range(2)
                ],
                axis=1,
            )
            filt_sums[:, half * 256 : half * 256 + 256] = mm(fwd_ref[...], data)

        return [lambda h=h: piece(h) for h in range(2)]

    def filter_twist():
        def piece(ks):
            found = [twist_forward([filt_sums], cos_ref, sin_ref, k)[0] for k in ks]
            store_rows(filt_z, ks[0] * 8, found)

        return [lambda ks=ks: piece(ks) for ks in [(k, k + 1) for k in range(0, A, 2)] + [(A,)]]

    def taps_rows():
        def piece(k):
            filt_z[k * 8 : k * 8 + 16, :] = taps_ref[k * 8 : k * 8 + 16, :].astype(BF)

        def last():
            filt_z[A * 8 :, :] = taps_ref[A * 8 :, :].astype(BF)

        return [lambda k=k: piece(k) for k in range(0, A, 2)] + [last]

    interleave(filter_sums() + block_sums(0), [])
    interleave(block_sums(1)[:2], filter_twist())
    interleave(row_sums(filt_z, fr_ref, filt_ref) + block_sums(1)[2:], forward_twist(0))
    for g in range(X):
        interleave(forward_rows(g), back_twists(g - 1) if g > 0 else [])
        interleave(results(g - 1) if g > 0 else [], products(g))
        interleave(back_rows(g), forward_twist(g + 1) if g + 1 < X else taps_rows())
        if g + 2 < X:
            interleave(block_sums(g + 2), [])
    interleave(row_sums(filt_z, ir_ref, filt_ref), back_twists(X - 1))
    interleave(results(X - 1), back_twist(filt_ref, 8, [u_ref.at[0, 0]]))

    result = mm(inv_ref[...], u_ref[0, 0]) * (1.0 / 256.0)
    place = lax.broadcasted_iota(jnp.int32, (A * 8, L), 0) % 8 // 2
    for g in range(4):
        total = result[:, :L] if g == 0 else pltpu.roll(result[:, :L], (-2 * g) % (A * 8), 0)
        for n in range(1, 4):
            part = result[:, n * L : (n + 1) * L]
            moved = part if n == g else pltpu.roll(part, (2 * (n - g)) % (A * 8), 0)
            total = jnp.where(place == n, moved, total)
        out_ref[:, g, 64:72, :] = total.reshape(A, 8, L).astype(BF)


def transform(fields, t):
    return pl.pallas_call(
        transform_kernel,
        out_shape=jax.ShapeDtypeStruct((A, X, ROWS, L), BF),
        in_specs=[whole()] * 7,
        out_specs=whole(),
        scratch_shapes=[
            pltpu.VMEM((2, 2, 2 * KH * 8, SEG), F32),
            pltpu.VMEM((2, KH * 16, 2 * SEG), BF),
            pltpu.VMEM((2, KH * 16, 2 * SEG), F32),
            pltpu.VMEM((2, KH * 16, 2 * SEG), BF),
            pltpu.VMEM((2, KH * 16, 2 * SEG), F32),
            pltpu.VMEM((2, 2, 2 * A * 8, SEG), BF),
            pltpu.VMEM((2 * KH * 8, SEG), F32),
            pltpu.VMEM((KH * 8, 2 * SEG), BF),
            pltpu.VMEM((KH * 8, 2 * SEG), F32),
            pltpu.VMEM((KH * 8, 2 * SEG), F32),
        ],
        compiler_params=pltpu.CompilerParams(vmem_limit_bytes=36 * MIB),
        name="transform",
    )(
        fields, t["forward"], t["backward"], t["fwd_rows"], t["inv_rows"],
        t["cos_twist"], t["sin_twist"],
    )


def finish_kernel(
    in_ref, q_ref, k_ref, v_ref, o_ref, skip_ref, order_ref,
    dq_hbm, dk_hbm, dv_hbm, df_hbm,
    dq_ref, dk_ref, dv_ref, df_ref, field_sems, taps_sem,
):
    def in_place(rows):
        return lax.dot_general(
            rows.astype(BF), order_ref[...], (((0,), (0,)), ((), ())), preferred_element_type=F32
        )

    copies = []
    for n in range(4):
        here = slice(n * L, (n + 1) * L)
        for half in range(2):
            part = up(in_ref[half * 64 : half * 64 + 64, n * 16 : n * 16 + 16, :])
            rows = jnp.concatenate(
                [part[:, :8].reshape(512, L), part[:, 8:].reshape(512, L)], axis=1
            )
            conv = in_place(rows)
            for g in range(4):
                cols = slice(g * 256 + half * 128, g * 256 + half * 128 + 128)
                state = conv[:L, g * L : (g + 1) * L]
                back = conv[L:, g * L : (g + 1) * L]
                q, k, v, o = (up(ref[here, cols]) for ref in (q_ref, k_ref, v_ref, o_ref))
                skip = skip_ref[:, cols]
                mixed = state + skip * up((k * v).astype(BF))
                total = back + skip * up((q * o).astype(BF))
                dq_ref[here, cols] = (o * mixed).astype(BF)
                dk_ref[here, cols] = (total * v).astype(BF)
                dv_ref[here, cols] = (total * k).astype(BF)
        if n == 1:
            for half in range(2):
                rows = up(in_ref[half * 64 : half * 64 + 64, 64:72, :]).reshape(512, L)
                taps = in_place(rows)
                for m in range(4):
                    df_ref[m * L : (m + 1) * L, half * 128 : half * 128 + 128] = taps[
                        :, m * L : (m + 1) * L
                    ]
            copies.append(pltpu.make_async_copy(df_ref, df_hbm, taps_sem))
            copies[-1].start()
        pairs = ((dq_ref, dq_hbm), (dk_ref, dk_hbm), (dv_ref, dv_hbm))
        for i, (source, target) in enumerate(pairs if n > 0 else ()):
            rows = pl.ds(0, 2 * L) if n == 1 else pl.ds(n * L, L)
            copies.append(
                pltpu.make_async_copy(source.at[rows], target.at[rows], field_sems.at[n, i])
            )
            copies[-1].start()
    for copy in copies:
        copy.wait()


def finish(fields, q_in, k_in, v_in, out_grad, skip, order):
    return pl.pallas_call(
        finish_kernel,
        out_shape=(
            jax.ShapeDtypeStruct((SEG, 1024), BF),
            jax.ShapeDtypeStruct((SEG, 1024), BF),
            jax.ShapeDtypeStruct((SEG, 1024), BF),
            jax.ShapeDtypeStruct((SEG, 256), F32),
        ),
        in_specs=[whole()] * 7,
        out_specs=(pl.BlockSpec(memory_space=pl.ANY),) * 4,
        scratch_shapes=[
            pltpu.VMEM((SEG, 1024), BF),
            pltpu.VMEM((SEG, 1024), BF),
            pltpu.VMEM((SEG, 1024), BF),
            pltpu.VMEM((SEG, 256), F32),
            pltpu.SemaphoreType.DMA((4, 3)),
            pltpu.SemaphoreType.DMA,
        ],
        compiler_params=pltpu.CompilerParams(vmem_limit_bytes=24 * MIB),
        name="finish",
    )(fields, q_in, k_in, v_in, out_grad, skip, order)


def body(q_in, k_in, v_in, out_grad, filters, skip):
    t = {name: jnp.asarray(value) for name, value in constants().items()}
    sent = pack(q_in, k_in, v_in, out_grad, filters)
    columns = lax.all_to_all(sent, ("ctx", "ch"), split_axis=0, concat_axis=0, tiled=True)
    results = transform(columns.reshape(A, X, ROWS, L), t)
    blocks = lax.all_to_all(
        results.reshape(DEV, ROWS, L), ("ctx", "ch"), split_axis=0, concat_axis=0, tiled=True
    )
    return finish(blocks, q_in, k_in, v_in, out_grad, skip.reshape(1, 1024), t["order"])


def solution(mesh):
    return jax.shard_map(
        body,
        mesh=mesh,
        in_specs=(
            P("ctx", "ch"),
            P("ctx", "ch"),
            P("ctx", "ch"),
            P("ctx", "ch"),
            P("ctx", None),
            P("ch"),
        ),
        out_specs=(P("ctx", "ch"), P("ctx", "ch"), P("ctx", "ch"), P("ctx", "ch")),
        check_vma=False,
    )
```
